32 devices in a mesh: parts: 2 (over y), seq: 4 (over z), head: 4 (over x, core).
Axes of the slice: x: 2, y: 2, z: 4, core: 2. Of those that a mesh axis runs over, the one named last changes fastest.
Arguments:
- xs: bfloat16 [8192, 5120], P(('parts', 'seq'), 'head'), parts along dimension 0, may hold values from -70 to 70
- gate_in: bfloat16 [8192, 5120], P(('parts', 'seq'), 'head'), parts along dimension 0, may hold values from -6 to 6
- bc_in: bfloat16 [8192, 256], P(('parts', 'seq')), parts along dimension 0, may hold values from -6 to 6
- dt_in: bfloat16 [8192, 64], P(('parts', 'seq'), 'head'), parts along dimension 0, may hold values from -3 to 3
- placement: int32 [8192], P(('parts', 'seq')), parts along dimension 0, may hold values from 0 to 4095, as said below
- lengths: int32 [6], P('parts'), parts along dimension 0, may hold values from 1 to 3072, 4096 in all
- conv_x: float32 [4, 5120], P(None, 'head'), may hold values from -3 to 3
- conv_bc: float32 [4, 256], replicated, may hold values from -3 to 3
- a_log: float32 [64], P('head'), may hold values from -9.5 to -0.5
- dt_bias: float32 [64], P('head'), may hold values from -3 to -1
- d_skip: float32 [64], P('head'), may hold values from 0.3 to 3
- norm_gain: float32 [5120], P('head'), may hold values from 0.1 to 1.9
Outputs:
- mixed: bfloat16 [8192, 5120], P(('parts', 'seq'), 'head'), parts along dimension 0
The draws below stay inside these ranges and needn't reach their ends.
There are 2 independent parts, one for each index of `parts`. The reference program is written for one: setup_inputs(seed, part) draws one part's arguments, and reference() takes and returns one part's arrays. A program takes and returns all parts, laid end to end along the dimension named above; an argument that names none is the same for every part. Nothing has to cross between parts.
Inputs may be any that keep to these rules, and one draw needn't show every extreme that they name: `placement`: A permutation of the packed positions; each ingest device holds exactly 1024 // 4 rows bound for every sequence shard. The lengths sum to 4096; the longest is 3072.
All inputs are finite; a program needn't handle non-finite values.
Results may differ from the reference program's by a relative error of at most 0.0025.
The reference program's roundings to bfloat16 on the way (of `convolved`) count: a program that leaves them out, or rounds other values in their place, can miss the bound.
Values may be sent and summed in bfloat16 or wider, within the bound.
No kernel may reach another device: no remote copies, remote signals or barrier semaphores. Data moves between devices by JAX's collectives and lax.ppermute only.
A program may use at most 128 MiB of HBM per device.

```python
import math
import jax
import jax.numpy as jnp
import numpy as np
from jax import lax

HEADS = 64
HEAD_DIM = 80
STATE = 128
KCONV = 4
BLOCK = 256
SEQS = 3
TOK_DEV = 1024
INNER = 5120
TOKENS = 4096


def draw_placement(key, part):
    shard_count = TOKENS // TOK_DEV
    share = TOK_DEV // shard_count
    first_keys = jax.random.split(jax.random.fold_in(key, 11), shard_count)
    orders = jax.vmap(lambda single: jax.random.permutation(single, TOK_DEV))(first_keys)
    slots = orders.astype(jnp.int32) + (jnp.arange(shard_count, dtype=jnp.int32) * TOK_DEV)[:, None]
    slots = slots.reshape(shard_count, shard_count, share).transpose(1, 0, 2).reshape(shard_count, TOK_DEV)
    second_keys = jax.random.split(jax.random.fold_in(key, 12), shard_count)
    shuffles = jax.vmap(lambda single: jax.random.permutation(single, TOK_DEV))(second_keys)
    slots = jnp.take_along_axis(slots, shuffles.astype(jnp.int32), axis=1)
    return slots.reshape(-1).astype(jnp.int32)


def draw_xs(key, part):
    columns = jnp.arange(INNER, dtype=jnp.float32) / INNER
    scales = 0.5 * jnp.power(10.0, columns)
    values = jnp.clip(jax.random.normal(key, (TOKENS, INNER), jnp.float32), -6.0, 6.0)
    return (values * scales[None, :]).astype(jnp.bfloat16)


def draw_a_log(key, part):
    return jax.random.uniform(key, (HEADS,), jnp.float32, -9.5, -0.5)


def level_of(rng, dims, cuts, least, largest):
    loudness, own = 1.0, jax.random.fold_in(rng, 6)
    for dim, shards_of in cuts:
        draws = jnp.exp(jax.random.uniform(jax.random.fold_in(own, dim), (shards_of,), jnp.float32, least / len(cuts), largest / len(cuts)))
        loudness = loudness * jnp.repeat(draws, dims[dim] // shards_of).reshape([-1 if axis == dim else 1 for axis in range(len(dims))])
    return loudness


def profile(amount, total, reach, slope):
    weights = [(1 << 20) // math.isqrt(grade ** slope) + 1 for grade in range(2, amount + 1)]
    rest, counts = total - reach - (amount - 1), [1] * (amount - 1)
    while rest > 0:
        movable = [i for i in range(amount - 1) if counts[i] < reach]
        whole, remaining = sum([weights[i] for i in movable]), rest
        for i in movable:
            extra = min(reach - counts[i], max(1, remaining * weights[i] // whole), rest)
            counts[i] = counts[i] + extra
            rest = rest - extra
    return np.array([reach] + counts)


def ragged(key, number_of, total, limit, slope):
    if number_of == 2:
        one = jax.random.randint(key, (), max(1, total - limit), min(limit, total - 1) + 1)
        return jnp.stack([one, total - one])
    sizes = jnp.asarray(profile(number_of, total, limit, slope), jnp.int32)
    twos = (number_of - 1) // 2
    giver, taker = sizes[1:1 + 2 * twos:2], sizes[2:2 + 2 * twos:2]
    margin = jnp.minimum(giver - 1, limit - taker)
    passed = jax.random.randint(jax.random.fold_in(key, 1), (twos,), 0, 1 << 20) % (margin + 1)
    sizes = sizes.at[1:1 + 2 * twos:2].set(giver - passed).at[2:2 + 2 * twos:2].set(taker + passed)
    return sizes[jax.random.permutation(jax.random.fold_in(key, 2), number_of)]


def centred(own_key, dims, scale, bound, shards=(), held_as=jnp.bfloat16):
    values = jax.random.normal(own_key, dims, jnp.float32) * scale
    if len(shards) > 0:
        values = level_of(own_key, dims, shards, -0.22, 0.18) * values
    return jnp.clip(values, min=-bound, max=bound).astype(held_as)


def setup_inputs(seed: int = 0, part: int = 0) -> dict:
    arg_keys = jax.random.split(jax.random.key(seed), 13)
    part_splits = jax.random.split(jax.random.fold_in(arg_keys[12], part), 13)
    return {
        "xs": draw_xs(jax.random.fold_in(jax.random.fold_in(arg_keys[12], part), 71), part),
        "gate_in": centred(part_splits[1], (TOKENS, INNER), 1.0, 6.0, ((0, 4), (1, 4))),
        "bc_in": centred(part_splits[2], (TOKENS, 2 * STATE), 1.0, 6.0, ((0, 4),)),
        "dt_in": centred(part_splits[3], (TOKENS, HEADS), 0.5, 3.0, ((0, 4), (1, 4))),
        "placement": draw_placement(jax.random.fold_in(jax.random.fold_in(arg_keys[12], part), 71), part),
        "lengths": ragged(part_splits[5], SEQS, TOKENS, 3 * TOKENS // 4, 2).astype(jnp.int32),
        "conv_x": centred(arg_keys[6], (KCONV, INNER), 0.5, 3.0, ((1, 4),), jnp.float32),
        "conv_bc": centred(arg_keys[7], (KCONV, 2 * STATE), 0.5, 3.0, (), jnp.float32),
        "a_log": draw_a_log(jax.random.fold_in(arg_keys[12], 71), part),
        "dt_bias": jnp.clip(-3.0 + 2.0 * jax.random.uniform(arg_keys[9], (HEADS,), jnp.float32) ** level_of(arg_keys[9], (HEADS,), ((0, 4),), -0.2, 0.2), -3.0, -1.0),
        "d_skip": jnp.clip(jnp.exp(math.log(3.0) - 2.3025851 * jax.random.uniform(arg_keys[10], (HEADS,), jnp.float32) ** level_of(arg_keys[10], (HEADS,), ((0, 4),), -0.2, 0.2)), 0.3, 3.0),
        "norm_gain": jnp.clip(1.0 + 0.18 * jax.random.normal(arg_keys[11], (INNER,), jnp.float32), 0.1, 1.9),
    }


highest = lax.Precision.HIGHEST

def convolve(rows, docs_rows, kernel):
    width = kernel.shape[0]
    count = rows.shape[0] - (width - 1)
    total = jnp.zeros((count, rows.shape[1]), jnp.float32)
    for lag in range(width):
        lower = width - 1 - lag
        match = (docs_rows[lower:lower + count] == docs_rows[width - 1:]).astype(jnp.float32)
        total = total + kernel[lag][None, :] * rows[lower:lower + count].astype(jnp.float32) * match[:, None]
    return jax.nn.silu(total).astype(jnp.bfloat16)

def block_pass(carry_state, pieces):
    conv_rows, key_rows, query_rows, step_sizes, log_decay, begins = pieces
    length = step_sizes.shape[0]
    head_count = step_sizes.shape[1]
    log_sums = jnp.cumsum(log_decay, axis=0)
    resets = jnp.cumsum(begins)
    places = jnp.arange(length)
    linked = (places[:, None] >= places[None, :]) & (resets[:, None] == resets[None, :])
    log_gaps = log_sums[:, None, :] - log_sums[None, :, :]
    weights = jnp.exp(jnp.where(linked[:, :, None], log_gaps, -jnp.inf))
    scores = jnp.dot(query_rows, key_rows.T, preferred_element_type=jnp.float32)
    mixing = scores[:, :, None] * weights * step_sizes[None, :, :]
    inputs = conv_rows.astype(jnp.float32).reshape(length, head_count, -1)
    outputs = jnp.einsum('tsh,shp->thp', mixing, inputs, precision=highest)
    carried = jnp.where((resets == 0)[:, None], jnp.exp(log_sums), 0.0)
    queries = query_rows.astype(jnp.float32)
    outputs = outputs + carried[:, :, None] * jnp.einsum('tn,hpn->thp', queries, carry_state, precision=highest)
    closing = jnp.where((resets == resets[-1])[:, None], jnp.exp(log_sums[-1][None, :] - log_sums), 0.0) * step_sizes
    key_values = key_rows.astype(jnp.float32)
    carry_state = carried[-1][:, None, None] * carry_state + jnp.einsum('sh,shp,sn->hpn', closing, inputs, key_values, precision=highest)
    return (carry_state, outputs.reshape(length, -1))

def reference(xs, gate_in, bc_in, dt_in, placement, lengths, conv_x, conv_bc, a_log, dt_bias, d_skip, norm_gain):
    packed_x = jnp.zeros_like(xs).at[placement].set(xs)
    packed_gate = jnp.zeros_like(gate_in).at[placement].set(gate_in)
    packed_bc = jnp.zeros_like(bc_in).at[placement].set(bc_in)
    packed_dt = jnp.zeros_like(dt_in).at[placement].set(dt_in)
    starts = (jnp.cumsum(lengths) - lengths).astype(jnp.int32)
    positions = jnp.arange(TOKENS + KCONV - 1, dtype=jnp.int32) - (KCONV - 1)
    docs = lax.optimization_barrier(jnp.sum((starts[None, :] <= positions[:, None]).astype(jnp.int32), axis=1)) - 1
    begin_all = lax.optimization_barrier(jnp.sum((starts[None, :] == positions[KCONV - 1:, None]).astype(jnp.int32), axis=1))
    channels = jnp.concatenate([packed_x, packed_bc], 1)
    padded = jnp.concatenate([jnp.zeros((KCONV - 1, channels.shape[1]), channels.dtype), channels], 0)
    kernel = jnp.concatenate([conv_x, conv_bc], 1)
    step_all = jax.nn.softplus(packed_dt.astype(jnp.float32) + dt_bias[None, :])
    decay_all = -jnp.exp(a_log)[None, :] * step_all

    def one_block(carry_state, block):
        first = (block * BLOCK).astype(jnp.int32)
        rows = lax.dynamic_slice_in_dim(padded, first, BLOCK + KCONV - 1, 0)
        docs_rows = lax.dynamic_slice_in_dim(docs, first, BLOCK + KCONV - 1, 0)
        convolved = convolve(rows, docs_rows, kernel)
        conv_rows = convolved[:, :INNER]
        key_rows = convolved[:, INNER:INNER + STATE]
        query_rows = convolved[:, INNER + STATE:]
        step_sizes = lax.dynamic_slice_in_dim(step_all, first, BLOCK, 0)
        log_decay = lax.dynamic_slice_in_dim(decay_all, first, BLOCK, 0)
        begins = lax.dynamic_slice_in_dim(begin_all, first, BLOCK, 0)
        carry_state, outputs = block_pass(carry_state, (conv_rows, key_rows, query_rows, step_sizes, log_decay, begins))
        inputs = conv_rows.astype(jnp.float32).reshape(BLOCK, HEADS, HEAD_DIM)
        outputs = outputs + (d_skip[None, :, None] * inputs).reshape(BLOCK, INNER)
        gates = lax.dynamic_slice_in_dim(packed_gate, first, BLOCK, 0)
        gated = outputs * jax.nn.silu(gates.astype(jnp.float32))
        mean_square = lax.optimization_barrier(jnp.sum(gated * gated, axis=1)) / INNER
        result = gated * lax.rsqrt(mean_square + 1e-05)[:, None] * norm_gain[None, :]
        return (carry_state, result.astype(jnp.bfloat16))
    empty = jnp.zeros((HEADS, HEAD_DIM, STATE), jnp.float32)
    blocks = jnp.arange(TOKENS // BLOCK, dtype=jnp.int32)
    final_state, results = lax.scan(one_block, empty, blocks)
    return results.reshape(TOKENS, INNER)
```

```python
import functools

import jax
import jax.numpy as jnp
from jax import lax
from jax.experimental import pallas as pl
from jax.experimental.pallas import tpu as pltpu
from jax.sharding import PartitionSpec as P

CHUNK = 64
ROWS = 256
TILE = 256
LANES = 128
RIM = 16
HALO = 8
GROUPS = 3
FAR = 1 << 28
bf16 = jnp.bfloat16
f32 = jnp.float32


def dot(a, b):
    return jnp.dot(a, b, preferred_element_type=f32)


def dot_nt(a, b):
    return lax.dot_general(a, b, (((1,), (1,)), ((), ())), preferred_element_type=f32)


def iota(shape, dim):
    return lax.broadcasted_iota(jnp.int32, shape, dim)


def ones_where(mask):
    return jnp.where(mask, 1.0, 0.0).astype(bf16)


def high_low(value):
    high = value.astype(bf16)
    return high, (value - high.astype(f32)).astype(bf16)


def split_lanes(value, heads):
    lane = iota(value.shape, 1)
    high = value.astype(bf16).astype(f32)
    rest = value - high
    middle = rest.astype(bf16).astype(f32)
    lowest = rest - middle
    pieces = jnp.where(lane < heads, high, jnp.where(lane < 2 * heads, middle, lowest))
    return jnp.where(lane < GROUPS * heads, pieces, 0.0).astype(bf16)


def silu(value):
    return value * jax.nn.sigmoid(value)


def call(kernel, outs, args, in_specs, out_specs, grid=(1,), scratch=(), flops=0, nbytes=0, limit=56):
    return pl.pallas_call(
        kernel,
        grid=grid,
        in_specs=in_specs,
        out_specs=out_specs,
        out_shape=outs,
        scratch_shapes=list(scratch),
        compiler_params=pltpu.CompilerParams(vmem_limit_bytes=limit * 1024 * 1024),
        cost_estimate=pl.CostEstimate(flops=flops, bytes_accessed=nbytes, transcendentals=0),
    )(*args)


def whole(array):
    rank = len(array.shape)
    return pl.BlockSpec(array.shape, lambda *_: (0,) * rank)


def columns(rows, width=TILE):
    return pl.BlockSpec((rows, width), lambda j: (0, j))


def smem():
    return pl.BlockSpec(memory_space=pltpu.SMEM)


def shape(*dims, dtype=bf16):
    return jax.ShapeDtypeStruct(dims, dtype)


def send_order(shards, width, info, place_ref, bc_ref, dt_ref, pick_ref, *small_refs):
    rows = place_ref.shape[1]
    per = rows // shards
    heads = dt_ref.shape[1]
    quarter = bc_ref.shape[1] // info[2]
    me, lane_group = info[0], info[1]
    place = place_ref[...]
    padded = max(8, shards)
    owner = iota((padded, rows), 0)
    first = owner * rows
    mine = (place >= first) & (place < first + rows)
    earlier = ones_where(iota((rows, rows), 0) < iota((rows, rows), 1))
    before = dot(ones_where(mine), earlier)
    relative = jnp.where(owner >= me, owner - me, owner - me + shards)
    target = before + (relative * per).astype(f32)
    target = jnp.sum(jnp.where(mine, target, 0.0), axis=0, keepdims=True).astype(jnp.int32)
    local = jnp.sum(jnp.where(mine, (place - first + 1).astype(f32), 0.0), axis=0, keepdims=True)
    high = jnp.floor(local * (1.0 / 64.0))
    low = local - 64.0 * high
    base_lane = quarter + heads
    line = iota((LANES, rows), 0)
    digits = jnp.where(line == base_lane, high, jnp.where(line == base_lane + 1, low, 0.0)).astype(bf16)
    from_bc = ones_where(
        (iota((bc_ref.shape[1], LANES), 0) == iota((bc_ref.shape[1], LANES), 1) + lane_group * quarter)
        & (iota((bc_ref.shape[1], LANES), 1) < quarter)
    )
    from_dt = ones_where(iota((heads, LANES), 0) + quarter == iota((heads, LANES), 1))
    payload = (dot(bc_ref[...], from_bc) + dot(dt_ref[...], from_dt)).astype(bf16)
    for k in range(shards):
        pick = ones_where(iota((per, rows), 0) + k * per == target)
        pick_ref[k * per : (k + 1) * per] = pick
        dest = jnp.where(me + k >= shards, me + k - shards, me + k)
        row = iota((RIM, rows), 0)
        rim = ones_where((row < width - 1) & (place == row + (dest * rows - (width - 1))))
        pick_ref[rows + k * RIM : rows + (k + 1) * RIM] = rim
        small_refs[k][:per] = (dot(pick, payload) + dot_nt(pick, digits)).astype(bf16)
        small_refs[k][per:] = (dot(rim, payload) + dot_nt(rim, digits)).astype(bf16)


def gather_rows(shards, with_rim, pick_ref, x_ref, *out_refs):
    rows = x_ref.shape[0]
    per = rows // shards
    values = x_ref[...]
    for k in range(shards):
        out_refs[k][:per] = dot(pick_ref[k * per : (k + 1) * per], values).astype(bf16)
    if with_rim:
        rims = dot(pick_ref[rows:], values).astype(bf16)
        for k in range(shards):
            out_refs[k][per:] = rims[k * RIM : (k + 1) * RIM]


def distance(position, info, seqs, limit):
    gap = limit
    for j in range(seqs):
        start = info[4 + j]
        gap = jnp.where(position >= start, jnp.minimum(gap, position - start), gap)
    return gap


def convolve(block_of, taps, gap, width):
    total = taps[0:1] * block_of(0)
    for lag in range(1, width):
        total = total + jnp.where(gap >= lag, taps[lag : lag + 1] * block_of(lag), 0.0)
    return silu(total).astype(bf16)


def prepare(
    shards, width, seqs, heads, head_dim,
    info, own_ref, all_ref, taps_ref, lines_ref,
    pick_ref, rims_ref, gap_ref, score_high_ref, score_low_ref, query_ref, kept_query_ref,
    keys_ref, inside_ref, outside_ref, carried_ref, expand_ref, factor_ref, rest_ref,
    packed, log_sums, steps,
):
    rows = pick_ref.shape[0]
    per = rows // shards
    group = per + RIM
    state = query_ref.shape[1]
    groups = all_ref.shape[0]
    quarter = 2 * state // groups
    base = info[3]
    own_main = jnp.concatenate([own_ref[k * group : k * group + per] for k in range(shards)], 0)
    own_rim = jnp.concatenate([own_ref[k * group + per : (k + 1) * group] for k in range(shards)], 0)
    lane = iota((8, LANES), 1)
    weights = jnp.where(lane == quarter + heads, 64.0, jnp.where(lane == quarter + heads + 1, 1.0, 0.0)).astype(bf16)
    slots = dot_nt(weights, own_main)[0:1].astype(jnp.int32) - 1
    rim_slots = dot_nt(weights, own_rim)[0:1].astype(jnp.int32) - 1 - (rows - (width - 1)) + HALO - (width - 1)
    rim_pick = ones_where(iota((RIM, shards * RIM), 0) == rim_slots)
    rims_ref[...] = rim_pick
    bc_main = jnp.zeros((rows, 2 * state), f32)
    bc_rim = jnp.zeros((shards * RIM, 2 * state), f32)
    for g in range(groups):
        spread = ones_where(
            (iota((LANES, 2 * state), 0) + g * quarter == iota((LANES, 2 * state), 1))
            & (iota((LANES, 2 * state), 0) < quarter)
        )
        for k in range(shards):
            pass
        main = jnp.concatenate([all_ref[g, k * group : k * group + per] for k in range(shards)], 0)
        rim = jnp.concatenate([all_ref[g, k * group + per : (k + 1) * group] for k in range(shards)], 0)
        bc_main = bc_main + dot(main, spread)
        bc_rim = bc_rim + dot(rim, spread)
    bc_main = bc_main.astype(bf16)
    packed[0:HALO] = dot(rim_pick, bc_rim.astype(bf16))[0:HALO]
    lane_of = iota((LANES, LANES), 0) - quarter
    wide = iota((LANES, LANES), 1)
    copy_dt = ones_where(
        (lane_of >= 0) & (lane_of < heads)
        & ((lane_of == wide) | (lane_of + heads == wide) | (lane_of + 2 * heads == wide))
    )
    decay_rate = -jnp.exp(lines_ref[1:2])
    row_in = iota((ROWS, ROWS), 0)
    col_in = iota((ROWS, ROWS), 1)
    same_chunk = (row_in // CHUNK) == (col_in // CHUNK)
    lower = same_chunk & (col_in <= row_in)
    sums = ones_where(lower)
    expand = iota((LANES, heads * head_dim), 0)
    head_of = jnp.where(expand >= 2 * heads, expand - 2 * heads, jnp.where(expand >= heads, expand - heads, expand))
    channel = iota((LANES, heads * head_dim), 1)
    expand = ones_where(
        (expand < GROUPS * heads) & (channel >= head_of * head_dim) & (channel < (head_of + 1) * head_dim)
    )
    expand_ref[...] = expand
    for b in range(rows // ROWS):
        here = slice(b * ROWS, (b + 1) * ROWS)
        pick = ones_where(iota((ROWS, rows), 0) + b * ROWS == slots)
        pick_ref[here] = pick
        packed[HALO + b * ROWS : HALO + (b + 1) * ROWS] = dot(pick, bc_main)
        raw = dot(pick, own_main).astype(bf16)
        step = jax.nn.softplus(dot(raw, copy_dt) + lines_ref[0:1])
        log_decay = decay_rate * step
        high = log_decay.astype(bf16)
        rest = log_decay - high.astype(f32)
        middle = rest.astype(bf16)
        lowest = (rest - middle.astype(f32)).astype(bf16)
        log_sums[here] = dot(sums, high) + dot(sums, middle) + dot(sums, lowest)
        steps[here] = step
    total = jnp.zeros((1, LANES), f32)
    chunks = rows // CHUNK
    factors = []
    pending = None
    for c in range(chunks):
        here = slice(c * CHUNK, (c + 1) * CHUNK)
        logs = log_sums[here]
        centre = logs[CHUNK // 2 - 1 : CHUNK // 2]
        last = logs[CHUNK - 1 : CHUNK]
        outside_ref[here] = split_lanes(jnp.exp(logs - centre), heads)
        inside_ref[here] = split_lanes(jnp.exp(centre - logs) * steps[here], heads)
        offset = iota((CHUNK, LANES), 0) + c * CHUNK
        gap = distance(offset + base, info, seqs, FAR)
        gap_ref[here] = gap
        carried_ref[here] = split_lanes(jnp.where(gap > offset, jnp.exp(logs + total), 0.0), heads)
        if pending is not None:
            factors.append(jnp.exp(pending + centre))
        pending = last - centre
        total = total + last
    factors.append(jnp.exp(pending))
    end_gap = distance(base + rows - 1, info, seqs, FAR)
    decay = jnp.where(end_gap >= rows, jnp.exp(total), 0.0)
    for c in range(chunks):
        log_sums[c : c + 1] = factors[c]
    factor_ref[...] = dot(split_lanes(log_sums[0:chunks], heads), expand)
    log_sums[0:1] = decay
    log_sums[1:2] = lines_ref[2:3]
    rest_ref[...] = dot(split_lanes(log_sums[0:8], heads), expand)
    for b in range(rows // ROWS):
        here = slice(b * ROWS, (b + 1) * ROWS)
        gap = gap_ref[here]
        wide_gap = jnp.concatenate([gap] * (2 * state // LANES), 1)

        def shifted(lag):
            return packed[HALO + b * ROWS - lag : HALO + (b + 1) * ROWS - lag]

        both = convolve(shifted, taps_ref[...], wide_gap, width)
        keys, queries = both[:, :state], both[:, state:]
        query_ref[here] = queries
        offset = iota((ROWS, state), 0)
        in_chunk = offset % CHUNK
        zero = jnp.zeros_like(queries)
        kept_query_ref[here] = jnp.where(gap > in_chunk, queries.astype(f32), 0.0).astype(bf16)
        ends = jnp.zeros((ROWS, state), jnp.int32)
        for c in range(ROWS // CHUNK):
            end = base + b * ROWS + (c + 1) * CHUNK - 1
            ends = jnp.where(offset // CHUNK == c, distance(end, info, seqs, FAR), ends)
        last_keys = jnp.where(CHUNK - 1 - in_chunk <= ends, keys.astype(f32), 0.0)
        keys_ref[:, here] = last_keys.T.astype(bf16)
        scores = dot_nt(queries, keys)
        gap_square = jnp.concatenate([gap] * (ROWS // LANES), 1)
        scores = jnp.where(lower & (row_in - col_in <= gap_square), scores, 0.0)
        high, low = high_low(scores)
        score_high_ref[here] = high
        score_low_ref[here] = low


def scan_columns(
    shards, width, seqs,
    info, pick_ref, rims_ref, gap_ref, score_high_ref, score_low_ref, kept_query_ref, keys_ref,
    inside_ref, outside_ref, expand_ref, factor_ref, rest_ref, taps_ref, *refs,
):
    blocks = refs[:shards]
    out_ref, state_ref, arrived, packed = refs[shards:]
    rows = pick_ref.shape[0]
    per = rows // shards
    base = info[3]
    for k in range(shards):
        arrived[k * per : (k + 1) * per] = blocks[k][:per]
    rim = jnp.concatenate([blocks[k][per:] for k in range(shards)], 0)
    packed[0:HALO] = dot(rims_ref[...], rim)[0:HALO]
    expand = expand_ref[...]
    state_ref[...] = jnp.zeros_like(state_ref)
    for b in range(rows // ROWS):
        here = slice(b * ROWS, (b + 1) * ROWS)
        packed[HALO + b * ROWS : HALO + (b + 1) * ROWS] = dot(pick_ref[here], arrived[...])
        gap = gap_ref[here]

        def shifted(lag):
            return packed[HALO + b * ROWS - lag : HALO + (b + 1) * ROWS - lag]

        conv = convolve(shifted, taps_ref[...], jnp.concatenate([gap] * (TILE // LANES), 1), width).astype(f32)
        scaled = conv * dot(inside_ref[here], expand)
        high, low = high_low(scaled)
        score_high, score_low = score_high_ref[here], score_low_ref[here]
        total = dot(score_high, high) + dot(score_low, high) + dot(score_high, low)
        outside = dot(outside_ref[here], expand)
        carry = state_ref[...]
        parts = []
        for c in range(ROWS // CHUNK):
            inner = slice(c * CHUNK, (c + 1) * CHUNK)
            place = slice(b * ROWS + c * CHUNK, b * ROWS + (c + 1) * CHUNK)
            carry_high, carry_low = high_low(carry)
            kept = kept_query_ref[place]
            parts.append(dot(kept, carry_high) + dot(kept, carry_low))
            keys = keys_ref[:, place]
            added = dot(keys, high[inner]) + dot(keys, low[inner])
            end = base + b * ROWS + (c + 1) * CHUNK - 1
            keep = jnp.where(distance(end, info, seqs, FAR) >= CHUNK, 1.0, 0.0)
            number = b * (ROWS // CHUNK) + c
            carry = (carry * keep + added) * factor_ref[number : number + 1]
        state_ref[...] = carry
        out_ref[here] = outside * (total + jnp.concatenate(parts, 0)) + rest_ref[1:2] * conv


def gate_columns(shards, pick_ref, query_ref, carried_ref, expand_ref, scan_ref, state_ref, *refs):
    blocks = refs[:shards]
    out_ref, square_ref, arrived = refs[shards:]
    rows = pick_ref.shape[0]
    per = rows // shards
    for k in range(shards):
        arrived[k * per : (k + 1) * per] = blocks[k][...]

    @pl.when(pl.program_id(0) == 0)
    def _():
        square_ref[...] = jnp.zeros_like(square_ref)

    carry_high, carry_low = high_low(state_ref[...])
    for b in range(rows // ROWS):
        here = slice(b * ROWS, (b + 1) * ROWS)
        gate = dot(pick_ref[here], arrived[...])
        queries = query_ref[here]
        earlier = dot(queries, carry_high) + dot(queries, carry_low)
        outputs = scan_ref[here] + dot(carried_ref[here], expand_ref[...]) * earlier
        gated = outputs * silu(gate)
        out_ref[here] = gated
        squares = gated * gated
        part = squares[:, :LANES]
        for piece in range(1, TILE // LANES):
            part = part + squares[:, piece * LANES : (piece + 1) * LANES]
        square_ref[here] = square_ref[here] + part


def exchanged(blocks, axis):
    count = lax.axis_size(axis)
    moved = [
        lax.ppermute(blocks[k], axis, [(i, (i + k) % count) for i in range(count)]) for k in range(1, count)
    ]
    return [blocks[0]] + moved


def body(xs, gate_in, bc_in, dt_in, placement, lengths, conv_x, conv_bc, a_log, dt_bias, d_skip, norm_gain):
    shards = lax.axis_size("seq")
    groups = lax.axis_size("head")
    rows, inner = xs.shape
    width, seqs = conv_x.shape[0], lengths.shape[0]
    heads = a_log.shape[0]
    head_dim = inner // heads
    state = bc_in.shape[1] // 2
    per = rows // shards
    group = per + RIM
    tiles = inner // TILE
    chunks = rows // CHUNK
    me = lax.axis_index("seq").astype(jnp.int32)
    starts = jnp.cumsum(lengths) - lengths
    info = jnp.concatenate(
        [
            jnp.stack([me, lax.axis_index("head").astype(jnp.int32), jnp.int32(groups), me * rows]),
            starts.astype(jnp.int32),
        ]
    )
    triple = jnp.stack([dt_bias, a_log, d_skip])
    lines = jnp.pad(jnp.concatenate([triple] * GROUPS, 1), ((0, 5), (0, LANES - GROUPS * heads)))

    place = placement.reshape(1, rows)
    full = rows + shards * RIM
    sent = call(
        functools.partial(send_order, shards, width),
        [shape(full, rows)] + [shape(group, LANES)] * shards,
        (info, place, bc_in, dt_in),
        [smem(), whole(place), whole(bc_in), whole(dt_in)],
        [whole(shape(full, rows))] + [whole(shape(group, LANES))] * shards,
        flops=2 * full * rows * LANES * 2,
        nbytes=2 * full * rows,
    )
    picks, small = sent[0], sent[1:]
    small = exchanged(small, "seq")
    own = jnp.concatenate(small, 0)
    every = lax.all_gather(own, "head")

    x_send = call(
        functools.partial(gather_rows, shards, True),
        [shape(group, inner)] * shards,
        (picks, xs),
        [whole(picks), columns(rows)],
        [columns(group)] * shards,
        grid=(tiles,),
        flops=2 * full * rows * inner,
        nbytes=2 * full * rows + 4 * rows * inner,
    )
    x_blocks = exchanged(x_send, "seq")
    gate_send = call(
        functools.partial(gather_rows, shards, False),
        [shape(per, inner)] * shards,
        (picks, gate_in),
        [pl.BlockSpec((rows, rows), lambda j: (0, 0)), columns(rows)],
        [columns(per)] * shards,
        grid=(tiles,),
        flops=2 * rows * rows * inner,
        nbytes=2 * rows * rows + 4 * rows * inner,
    )

    kept = [
        shape(rows, rows),
        shape(RIM, shards * RIM),
        shape(rows, LANES, dtype=jnp.int32),
        shape(rows, ROWS),
        shape(rows, ROWS),
        shape(rows, state),
        shape(rows, state),
        shape(state, rows),
        shape(rows, LANES),
        shape(rows, LANES),
        shape(rows, LANES),
        shape(LANES, inner),
        shape(chunks, inner, dtype=f32),
        shape(8, inner, dtype=f32),
    ]
    (
        pick, rims, gap, score_high, score_low, query, kept_query,
        keys, inside, outside, carried, expand, factor, rest,
    ) = call(
        functools.partial(prepare, shards, width, seqs, heads, head_dim),
        kept,
        (info, own, every, conv_bc, lines),
        [smem(), whole(own), whole(every), whole(conv_bc), whole(lines)],
        [whole(s) for s in kept],
        scratch=[
            pltpu.VMEM((rows + HALO, 2 * state), f32),
            pltpu.VMEM((rows, LANES), f32),
            pltpu.VMEM((rows, LANES), f32),
        ],
        flops=2 * rows * rows * 4 * LANES,
        nbytes=2 * rows * rows,
    )

    gate_send, x_blocks = lax.optimization_barrier((gate_send, x_blocks))
    gate_blocks = exchanged(gate_send, "seq")

    scanned, local_state = call(
        functools.partial(scan_columns, shards, width, seqs),
        [shape(rows, inner, dtype=f32), shape(state, inner, dtype=f32)],
        (
            info, pick, rims, gap, score_high, score_low, kept_query, keys, inside, outside,
            expand, factor, rest, conv_x, *x_blocks,
        ),
        [smem()]
        + [whole(a) for a in (pick, rims, gap, score_high, score_low, kept_query, keys, inside, outside)]
        + [columns(LANES), columns(chunks), columns(8), columns(width)]
        + [columns(group)] * shards,
        [columns(rows), columns(state)],
        grid=(tiles,),
        scratch=[pltpu.VMEM((rows, TILE), bf16), pltpu.VMEM((rows + HALO, TILE), f32)],
        flops=2 * rows * inner * (rows + 8 * ROWS),
        nbytes=10 * rows * inner,
    )

    incoming = jnp.zeros((state, inner), f32)
    for step in range(1, shards):
        leaving = local_state + rest[0:1] * incoming
        incoming = incoming + lax.ppermute(leaving, "seq", [(step - 1, step)])

    gated, squares = call(
        functools.partial(gate_columns, shards),
        [shape(rows, inner, dtype=f32), shape(rows, LANES, dtype=f32)],
        (pick, query, carried, expand, scanned, incoming, *gate_blocks),
        [whole(pick), whole(query), whole(carried), columns(LANES), columns(rows), columns(state)]
        + [columns(per)] * shards,
        [columns(rows), pl.BlockSpec((rows, LANES), lambda j: (0, 0))],
        grid=(tiles,),
        scratch=[pltpu.VMEM((rows, TILE), bf16)],
        flops=2 * rows * inner * (rows + 3 * ROWS),
        nbytes=12 * rows * inner,
    )
    mean = lax.psum(jnp.sum(squares, axis=1), "head") / (inner * groups)
    result = gated * lax.rsqrt(mean + 1e-05)[:, None] * norm_gain[None, :]
    return result.astype(jnp.bfloat16)


def solution(mesh):
    in_specs = (
        P(("parts", "seq"), "head"),
        P(("parts", "seq"), "head"),
        P(("parts", "seq"), None),
        P(("parts", "seq"), "head"),
        P(("parts", "seq")),
        P("parts"),
        P(None, "head"),
        P(),
        P("head"),
        P("head"),
        P("head"),
        P("head"),
    )
    out_specs = P(("parts", "seq"), "head")
    return jax.shard_map(body, mesh=mesh, in_specs=in_specs, out_specs=out_specs, check_vma=False)
```

```python
import functools

import jax
import jax.numpy as jnp
from jax import lax
from jax.experimental import pallas as pl
from jax.experimental.pallas import tpu as pltpu
from jax.sharding import PartitionSpec as P

CHUNK = 64
ROWS = 256
TILE = 256
LANES = 128
RIM = 16
SHARES = (0.4, 0.8)
GATE_SHARES = (0.4, 0.8)
HALO = 8
GROUPS = 3
FAR = 1 << 28
FLOPS_US = 1_150_000_000
bf16 = jnp.bfloat16
f32 = jnp.float32


def dot(a, b):
    return jnp.dot(a, b, preferred_element_type=f32)


def dot_nt(a, b):
    return lax.dot_general(a, b, (((1,), (1,)), ((), ())), preferred_element_type=f32)


def iota(shape, dim):
    return lax.broadcasted_iota(jnp.int32, shape, dim)


def ones_where(mask):
    return jnp.where(mask, 1.0, 0.0).astype(bf16)


def high_low(value):
    high = value.astype(bf16)
    return high, (value - high.astype(f32)).astype(bf16)


def split_lanes(value, heads):
    lane = iota(value.shape, 1)
    high = value.astype(bf16).astype(f32)
    rest = value - high
    middle = rest.astype(bf16).astype(f32)
    lowest = rest - middle
    pieces = jnp.where(lane < heads, high, jnp.where(lane < 2 * heads, middle, lowest))
    return jnp.where(lane < GROUPS * heads, pieces, 0.0).astype(bf16)


def silu(value):
    return value * jax.nn.sigmoid(value)


def call(kernel, outs, args, in_specs, out_specs, grid=(1,), scratch=(), micros=1, limit=24):
    return pl.pallas_call(
        kernel,
        grid=grid,
        in_specs=in_specs,
        out_specs=out_specs,
        out_shape=outs,
        scratch_shapes=list(scratch),
        compiler_params=pltpu.CompilerParams(vmem_limit_bytes=limit * 1024 * 1024),
        cost_estimate=pl.CostEstimate(flops=int(micros * FLOPS_US), bytes_accessed=0, transcendentals=0),
    )(*args)


def whole(array):
    rank = len(array.shape)
    return pl.BlockSpec(array.shape, lambda *_: (0,) * rank)


def columns(rows, width=TILE, start=0):
    return pl.BlockSpec((rows, width), lambda j: (0, j + start))


def smem():
    return pl.BlockSpec(memory_space=pltpu.SMEM)


def shape(*dims, dtype=bf16):
    return jax.ShapeDtypeStruct(dims, dtype)


def send_order(shards, width, place_ref, bc_ref, dt_ref, x_ref, pick_ref, *refs):
    small_refs, x_refs = refs[:shards], refs[shards:]
    rows = place_ref.shape[1]
    per = rows // shards
    heads = dt_ref.shape[0]
    wide = bc_ref.shape[1]

    @pl.when(pl.program_id(0) == 0)
    def _():
        me = lax.axis_index("seq")
        place = place_ref[...]
        padded = max(8, shards)
        owner = iota((padded, rows), 0)
        first = owner * rows
        mine = (place >= first) & (place < first + rows)
        chosen = ones_where(mine)
        earlier = ones_where(iota((LANES, LANES), 0) < iota((LANES, LANES), 1))
        before, seen = [], jnp.zeros((padded, 1), f32)
        for piece in range(rows // LANES):
            part = chosen[:, piece * LANES : (piece + 1) * LANES]
            before.append(dot(part, earlier) + seen)
            seen = seen + jnp.sum(part.astype(f32), axis=1, keepdims=True)
        before = jnp.concatenate(before, 1)
        relative = jnp.where(owner >= me, owner - me, owner - me + shards)
        target = before + (relative * per).astype(f32)
        target = jnp.sum(jnp.where(mine, target, 0.0), axis=0, keepdims=True).astype(jnp.int32)
        local = jnp.sum(jnp.where(mine, (place - first + 1).astype(f32), 0.0), axis=0, keepdims=True)
        high = jnp.floor(local * (1.0 / 64.0))
        low = local - 64.0 * high
        line = iota((LANES - heads, rows), 0)
        digits = jnp.where(line == 0, high, jnp.where(line == 1, low, 0.0)).astype(bf16)
        thin = jnp.concatenate([dt_ref[...], digits], 0)
        for k in range(shards):
            pick = ones_where(iota((per, rows), 0) + k * per == target)
            pick_ref[k * per : (k + 1) * per] = pick
            dest = jnp.where(me + k >= shards, me + k - shards, me + k)
            row = iota((RIM, rows), 0)
            rim = ones_where((row < width - 1) & (place == row + (dest * rows - (width - 1))))
            pick_ref[rows + k * RIM : rows + (k + 1) * RIM] = rim
            small_refs[k][:per, :wide] = dot(pick, bc_ref[...]).astype(bf16)
            small_refs[k][per:, :wide] = dot(rim, bc_ref[...]).astype(bf16)
            small_refs[k][:per, wide:] = dot_nt(pick, thin).astype(bf16)
            small_refs[k][per:, wide:] = dot_nt(rim, thin).astype(bf16)

    gather_rows(shards, True, pick_ref, x_ref, *x_refs)


def gather_rows(shards, with_rim, pick_ref, x_ref, *out_refs):
    rows = x_ref.shape[0]
    per = rows // shards
    values = x_ref[...]
    for k in range(shards):
        out_refs[k][:per] = dot(pick_ref[k * per : (k + 1) * per], values).astype(bf16)
    if with_rim:
        rims = dot(pick_ref[rows:], values).astype(bf16)
        for k in range(shards):
            out_refs[k][per:] = rims[k * RIM : (k + 1) * RIM]


def gather_parts(shards, parts, pick_ref, x_ref, *out_refs):
    rows = x_ref.shape[0]
    per = rows // shards
    values = x_ref[...]
    for number, (first, last) in enumerate(parts):

        @pl.when((pl.program_id(0) >= first) & (pl.program_id(0) < last))
        def _():
            for k in range(shards):
                taken = dot(pick_ref[k * per : (k + 1) * per], values)
                out_refs[number * shards + k][...] = taken.astype(bf16)


def distance(position, lengths, limit):
    gap, start = limit, 0
    for j in range(lengths.shape[0]):
        gap = jnp.where(position >= start, jnp.minimum(gap, position - start), gap)
        start = start + lengths[j]
    return gap


def convolve(block_of, taps, gap, width):
    total = taps[0:1] * block_of(0)
    for lag in range(1, width):
        total = total + jnp.where(gap >= lag, taps[lag : lag + 1] * block_of(lag), 0.0)
    return silu(total).astype(bf16)


def prepare(
    shards, width, heads, head_dim, lengths, *refs
):
    own_refs = refs[:shards]
    (
        taps_ref, lines_ref,
        pick_ref, rims_ref, gap_ref, score_high_ref, score_low_ref, query_ref, kept_query_ref,
        keys_ref, inside_ref, outside_ref, carried_ref, expand_ref, factor_ref, rest_ref,
        packed, log_sums, steps,
    ) = refs[shards:]
    rows = pick_ref.shape[0]
    per = rows // shards
    state = query_ref.shape[1]
    base = lax.axis_index("seq") * rows
    own_main = jnp.concatenate([ref[:per] for ref in own_refs], 0)
    own_rim = jnp.concatenate([ref[per:] for ref in own_refs], 0)
    lane = iota((8, LANES), 1)
    weights = jnp.where(lane == heads, 64.0, jnp.where(lane == heads + 1, 1.0, 0.0)).astype(bf16)
    slots = dot_nt(weights, own_main[:, 2 * state :])[0:1].astype(jnp.int32) - 1
    rim_slots = dot_nt(weights, own_rim[:, 2 * state :])[0:1].astype(jnp.int32) - 1 - rows + HALO
    rim_pick = ones_where(iota((RIM, shards * RIM), 0) == rim_slots)
    rims_ref[...] = rim_pick
    bc_main = own_main[:, : 2 * state]
    own_main = own_main[:, 2 * state :]
    packed[0:HALO] = dot(rim_pick, own_rim[:, : 2 * state])[0:HALO]
    lane_of = iota((LANES, LANES), 0)
    wide = iota((LANES, LANES), 1)
    copy_dt = ones_where(
        (lane_of < heads)
        & ((lane_of == wide) | (lane_of + heads == wide) | (lane_of + 2 * heads == wide))
    )
    decay_rate = -jnp.exp(lines_ref[1:2])
    row_in = iota((ROWS, ROWS), 0)
    col_in = iota((ROWS, ROWS), 1)
    same_chunk = (row_in // CHUNK) == (col_in // CHUNK)
    lower = same_chunk & (col_in <= row_in)
    sums = ones_where(lower)
    expand = iota((LANES, heads * head_dim), 0)
    head_of = jnp.where(expand >= 2 * heads, expand - 2 * heads, jnp.where(expand >= heads, expand - heads, expand))
    channel = iota((LANES, heads * head_dim), 1)
    expand = ones_where(
        (expand < GROUPS * heads) & (channel >= head_of * head_dim) & (channel < (head_of + 1) * head_dim)
    )
    expand_ref[...] = expand
    for b in range(rows // ROWS):
        here = slice(b * ROWS, (b + 1) * ROWS)
        pick = ones_where(iota((ROWS, rows), 0) + b * ROWS == slots)
        pick_ref[here] = pick
        packed[HALO + b * ROWS : HALO + (b + 1) * ROWS] = dot(pick, bc_main)
        raw = dot(pick, own_main).astype(bf16)
        step = jax.nn.softplus(dot(raw, copy_dt) + lines_ref[0:1])
        log_decay = decay_rate * step
        high = log_decay.astype(bf16)
        rest = log_decay - high.astype(f32)
        middle = rest.astype(bf16)
        lowest = (rest - middle.astype(f32)).astype(bf16)
        log_sums[here] = dot(sums, high) + dot(sums, middle) + dot(sums, lowest)
        steps[here] = step
    total = jnp.zeros((1, LANES), f32)
    chunks = rows // CHUNK
    factors = []
    pending = None
    for c in range(chunks):
        here = slice(c * CHUNK, (c + 1) * CHUNK)
        logs = log_sums[here]
        centre = logs[CHUNK // 2 - 1 : CHUNK // 2]
        last = logs[CHUNK - 1 : CHUNK]
        outside_ref[here] = split_lanes(jnp.exp(logs - centre), heads)
        inside_ref[here] = split_lanes(jnp.exp(centre - logs) * steps[here], heads)
        offset = iota((CHUNK, LANES), 0) + c * CHUNK
        gap = distance(offset + base, lengths, FAR)
        gap_ref[here] = gap
        carried_ref[here] = split_lanes(jnp.where(gap > offset, jnp.exp(logs + total), 0.0), heads)
        if pending is not None:
            factors.append(jnp.exp(pending + centre))
        pending = last - centre
        total = total + last
    factors.append(jnp.exp(pending))
    end_gap = distance(base + rows - 1, lengths, FAR)
    decay = jnp.where(end_gap >= rows, jnp.exp(total), 0.0)
    for c in range(chunks):
        log_sums[c : c + 1] = factors[c]
    factor_ref[...] = dot(split_lanes(log_sums[0:chunks], heads), expand)
    log_sums[0:1] = decay
    log_sums[1:2] = lines_ref[2:3]
    rest_ref[...] = dot(split_lanes(log_sums[0:8], heads), expand)
    for b in range(rows // ROWS):
        here = slice(b * ROWS, (b + 1) * ROWS)
        gap = gap_ref[here]
        wide_gap = jnp.concatenate([gap] * (2 * state // LANES), 1)

        def shifted(lag):
            return packed[HALO + b * ROWS - lag : HALO + (b + 1) * ROWS - lag]

        both = convolve(shifted, taps_ref[...], wide_gap, width)
        keys, queries = both[:, :state], both[:, state:]
        query_ref[here] = queries
        offset = iota((ROWS, state), 0)
        in_chunk = offset % CHUNK
        zero = jnp.zeros_like(queries)
        kept_query_ref[here] = jnp.where(gap > in_chunk, queries.astype(f32), 0.0).astype(bf16)
        ends = jnp.zeros((ROWS, state), jnp.int32)
        for c in range(ROWS // CHUNK):
            end = base + b * ROWS + (c + 1) * CHUNK - 1
            ends = jnp.where(offset // CHUNK == c, distance(end, lengths, FAR), ends)
        last_keys = jnp.where(CHUNK - 1 - in_chunk <= ends, keys.astype(f32), 0.0)
        keys_ref[:, here] = last_keys.T.astype(bf16)
        scores = dot_nt(queries, keys)
        gap_square = jnp.concatenate([gap] * (ROWS // LANES), 1)
        scores = jnp.where(lower & (row_in - col_in <= gap_square), scores, 0.0)
        high, low = high_low(scores)
        score_high_ref[here] = high
        score_low_ref[here] = low


def scan_columns(
    shards, width,
    lengths, pick_ref, rims_ref, gap_ref, score_high_ref, score_low_ref, kept_query_ref, keys_ref,
    inside_ref, outside_ref, expand_ref, factor_ref, rest_ref, taps_ref, *refs,
):
    blocks = refs[:shards]
    out_ref, state_ref, arrived, packed = refs[shards:]
    rows = pick_ref.shape[0]
    per = rows // shards
    base = lax.axis_index("seq") * rows
    for k in range(shards):
        arrived[k * per : (k + 1) * per] = blocks[k][:per]
    rim = jnp.concatenate([blocks[k][per:] for k in range(shards)], 0)
    packed[0:HALO] = dot(rims_ref[...], rim)[0:HALO]
    expand = expand_ref[...]
    state_ref[...] = jnp.zeros_like(state_ref)
    for b in range(rows // ROWS):
        here = slice(b * ROWS, (b + 1) * ROWS)
        packed[HALO + b * ROWS : HALO + (b + 1) * ROWS] = dot(pick_ref[here], arrived[...])
        gap = gap_ref[here]

        def shifted(lag):
            return packed[HALO + b * ROWS - lag : HALO + (b + 1) * ROWS - lag]

        conv = convolve(shifted, taps_ref[...], jnp.concatenate([gap] * (TILE // LANES), 1), width).astype(f32)
        scaled = conv * dot(inside_ref[here], expand)
        high, low = high_low(scaled)
        score_high, score_low = score_high_ref[here], score_low_ref[here]
        total = dot(score_high, high) + dot(score_low, high) + dot(score_high, low)
        outside = dot(outside_ref[here], expand)
        carry = state_ref[...]
        parts = []
        for c in range(ROWS // CHUNK):
            inner = slice(c * CHUNK, (c + 1) * CHUNK)
            place = slice(b * ROWS + c * CHUNK, b * ROWS + (c + 1) * CHUNK)
            carry_high, carry_low = high_low(carry)
            kept = kept_query_ref[place]
            parts.append(dot(kept, carry_high) + dot(kept, carry_low))
            keys = keys_ref[:, place]
            added = dot(keys, high[inner]) + dot(keys, low[inner])
            end = base + b * ROWS + (c + 1) * CHUNK - 1
            keep = jnp.where(distance(end, lengths, FAR) >= CHUNK, 1.0, 0.0)
            number = b * (ROWS // CHUNK) + c
            carry = (carry * keep + added) * factor_ref[number : number + 1]
        state_ref[...] = carry
        out_ref[here] = outside * (total + jnp.concatenate(parts, 0)) + rest_ref[1:2] * conv


def gate_columns(shards, pick_ref, query_ref, carried_ref, expand_ref, scan_ref, state_ref, *refs):
    blocks = refs[:shards]
    out_ref, total_ref, arrived, square_ref = refs[shards:]
    rows = pick_ref.shape[0]
    per = rows // shards
    for k in range(shards):
        arrived[k * per : (k + 1) * per] = blocks[k][...]

    @pl.when(pl.program_id(0) == 0)
    def _():
        square_ref[...] = jnp.zeros_like(square_ref)

    carry_high, carry_low = high_low(state_ref[...])
    for b in range(rows // ROWS):
        here = slice(b * ROWS, (b + 1) * ROWS)
        gate = dot(pick_ref[here], arrived[...])
        queries = query_ref[here]
        earlier = dot(queries, carry_high) + dot(queries, carry_low)
        outputs = scan_ref[here] + dot(carried_ref[here], expand_ref[...]) * earlier
        gated = outputs * silu(gate)
        out_ref[here] = gated
        squares = gated * gated
        part = squares[:, :LANES]
        for piece in range(1, TILE // LANES):
            part = part + squares[:, piece * LANES : (piece + 1) * LANES]
        square_ref[here] = square_ref[here] + part

    @pl.when(pl.program_id(0) == pl.num_programs(0) - 1)
    def _():
        for b in range(rows // ROWS):
            here = slice(b * ROWS, (b + 1) * ROWS)
            total_ref[:, here] = jnp.sum(square_ref[here].T, axis=0, keepdims=True)


def normalize(count, total_ref, gain_ref, *refs):
    pieces, out_ref = refs[:-1], refs[-1]
    scale = lax.rsqrt(total_ref[...] / count + 1e-05)
    scale = jnp.broadcast_to(scale, (LANES, scale.shape[1])).T
    first = 0
    for ref in pieces:
        for tile in range(ref.shape[1] // LANES):
            here = slice(first + tile * LANES, first + (tile + 1) * LANES)
            value = ref[:, tile * LANES : (tile + 1) * LANES] * scale * gain_ref[:, here]
            out_ref[:, here] = value.astype(bf16)
        first += ref.shape[1]


def moved(block, axis, steps):
    count = lax.axis_size(axis)
    return lax.ppermute(block, axis, [(i, (i + steps) % count) for i in range(count)])


def after(value, *others):
    return lax.optimization_barrier((value, *others))[0]


def cut(tiles, shares):
    cuts = sorted({0, *(round(tiles * share) for share in shares), tiles})
    return list(zip(cuts, cuts[1:]))


def body(xs, gate_in, bc_in, dt_in, placement, lengths, conv_x, conv_bc, a_log, dt_bias, d_skip, norm_gain):
    shards = lax.axis_size("seq")
    groups = lax.axis_size("head")
    rows, inner = xs.shape
    width = conv_x.shape[0]
    heads = a_log.shape[0]
    head_dim = inner // heads
    state = bc_in.shape[1] // 2
    per = rows // shards
    group = per + RIM
    tiles = inner // TILE
    chunks = rows // CHUNK
    parts = cut(tiles, SHARES)
    gate_parts = cut(tiles, GATE_SHARES)
    triple = jnp.stack([dt_bias, a_log, d_skip])
    lines = jnp.pad(jnp.concatenate([triple] * GROUPS, 1), ((0, 5), (0, LANES - GROUPS * heads)))

    place = placement.reshape(1, rows)
    thin = dt_in.T
    full = rows + shards * RIM
    thick = 2 * state + LANES
    first, last = parts[0]
    sent = call(
        functools.partial(send_order, shards, width),
        [shape(full, rows)] + [shape(group, thick)] * shards + [shape(group, (last - first) * TILE)] * shards,
        (place, bc_in, thin, xs),
        [whole(place), whole(bc_in), whole(thin), columns(rows)],
        [whole(shape(full, rows))] + [whole(shape(group, thick))] * shards + [columns(group)] * shards,
        grid=(last - first,),
        micros=7,
    )
    picks, small, x_send = sent[0], sent[1 : 1 + shards], [sent[1 + shards :]]
    small = [small[0]] + [moved(small[k], "seq", k) for k in range(1, shards)]
    arrived = [[x_send[0][0]] + [moved(x_send[0][k], "seq", k) for k in range(1, shards)]]

    for first, last in parts[1:]:
        x_send.append(
            call(
                functools.partial(gather_rows, shards, True),
                [shape(group, (last - first) * TILE)] * shards,
                (picks, xs),
                [whole(picks), columns(rows, start=first)],
                [columns(group)] * shards,
                grid=(last - first,),
                micros=2 * (last - first),
            )
        )
    def within(first, last):
        return pl.BlockSpec((per, TILE), lambda j: (0, jnp.clip(j - first, 0, last - first - 1)))

    gate_send = call(
        functools.partial(gather_parts, shards, gate_parts),
        [shape(per, (last - first) * TILE) for first, last in gate_parts for _ in range(shards)],
        (picks, gate_in),
        [whole(shape(rows, rows)), columns(rows)],
        [within(first, last) for first, last in gate_parts for _ in range(shards)],
        grid=(tiles,),
        micros=2 * tiles,
    )
    gate_send = [gate_send[number * shards : (number + 1) * shards] for number in range(len(gate_parts))]

    kept = [
        shape(rows, rows),
        shape(RIM, shards * RIM),
        shape(rows, LANES, dtype=jnp.int32),
        shape(rows, ROWS),
        shape(rows, ROWS),
        shape(rows, state),
        shape(rows, state),
        shape(state, rows),
        shape(rows, LANES),
        shape(rows, LANES),
        shape(rows, LANES),
        shape(LANES, inner),
        shape(chunks, inner, dtype=f32),
        shape(8, inner, dtype=f32),
    ]
    (
        pick, rims, gap, score_high, score_low, query, kept_query,
        keys, inside, outside, carried, expand, factor, rest,
    ) = call(
        functools.partial(prepare, shards, width, heads, head_dim),
        kept,
        (lengths, *small, conv_bc, lines),
        [smem()] + [whole(s) for s in small] + [whole(conv_bc), whole(lines)],
        [whole(s) for s in kept],
        scratch=[
            pltpu.VMEM((rows + HALO, 2 * state), f32),
            pltpu.VMEM((rows, LANES), f32),
            pltpu.VMEM((rows, LANES), f32),
        ],
        micros=8,
    )

    def stream(send, before, *others):
        return [send[0]] + [
            moved(after(send[k], before[k], *others), "seq", k) for k in range(1, shards)
        ]

    if len(parts) > 1:
        arrived.append(stream(x_send[1], arrived[0], rims, gate_send[0][0], x_send[-1][0]))

    scans, ends, states, gates = [], [], [], []
    for number, part in enumerate(parts):
        blocks = arrived[number]
        first, last = part
        size = (last - first) * TILE
        if ends:
            blocks = [after(blocks[0], ends[-1])] + blocks[1:]
        scanned, local_state = call(
            functools.partial(scan_columns, shards, width),
            [shape(rows, size, dtype=f32), shape(state, size, dtype=f32)],
            (
                lengths, pick, rims, gap, score_high, score_low, kept_query, keys, inside, outside,
                expand, factor, rest, conv_x, *blocks,
            ),
            [smem()]
            + [whole(a) for a in (pick, rims, gap, score_high, score_low, kept_query, keys, inside, outside)]
            + [columns(n, start=first) for n in (LANES, chunks, 8, width)]
            + [columns(group)] * shards,
            [columns(rows), columns(state)],
            grid=(last - first,),
            scratch=[pltpu.VMEM((rows, TILE), bf16), pltpu.VMEM((rows + HALO, TILE), f32)],
            micros=5 * (last - first),
        )
        scans.append(scanned)
        ends.append(local_state)
        if number + 2 < len(parts):
            arrived.append(stream(x_send[number + 2], arrived[number + 1], local_state))
        if not gates and number + 2 >= len(parts):
            gates.append(stream(gate_send[0], arrived[-1], local_state))
            for send in gate_send[1:]:
                gates.append(stream(send, gates[-1]))
        following = (arrived + gates)[number + 1]
        incoming = leaving = None
        for step in range(1, shards):
            leaving = after(local_state, following[1])
            if incoming is not None:
                leaving = leaving + rest[0:1, first * TILE : last * TILE] * incoming
            received = lax.ppermute(leaving, "seq", [(step - 1, step)])
            incoming = received if incoming is None else incoming + received
        states.append(incoming)

    outs, totals = [], []
    for tile in range(tiles):
        part = sum(tile >= last for _, last in parts)
        gate_part = sum(tile >= last for _, last in gate_parts)
        blocks = gates[gate_part]
        if gate_part + 1 < len(gates):
            blocks = [after(blocks[0], gates[gate_part + 1][1])] + blocks[1:]
        gated, total = call(
            functools.partial(gate_columns, shards),
            [shape(rows, TILE, dtype=f32), shape(1, rows, dtype=f32)],
            (pick, query, carried, expand, scans[part], states[part], *blocks),
            [whole(pick), whole(query), whole(carried), columns(LANES, start=tile)]
            + [columns(n, start=tile - parts[part][0]) for n in (rows, state)]
            + [columns(per, start=tile - gate_parts[gate_part][0])] * shards,
            [columns(rows), whole(shape(1, rows))],
            scratch=[pltpu.VMEM((rows, TILE), bf16), pltpu.VMEM((rows, LANES), f32)],
            micros=3,
        )
        outs.append(gated)
        totals.append(total)
    total = lax.psum(sum(totals), "head")
    gain = norm_gain.reshape(1, inner)
    return call(
        functools.partial(normalize, inner * groups),
        shape(rows, inner),
        (total, gain, *outs),
        [pl.BlockSpec((1, ROWS), lambda i: (0, i)), whole(gain)]
        + [pl.BlockSpec((ROWS, out.shape[1]), lambda i: (i, 0)) for out in outs],
        pl.BlockSpec((ROWS, inner), lambda i: (i, 0)),
        grid=(rows // ROWS,),
        micros=5,
    )


def solution(mesh):
    in_specs = (
        P(("parts", "seq"), "head"),
        P(("parts", "seq"), "head"),
        P(("parts", "seq"), None),
        P(("parts", "seq"), "head"),
        P(("parts", "seq")),
        P("parts"),
        P(None, "head"),
        P(),
        P("head"),
        P("head"),
        P("head"),
        P("head"),
    )
    out_specs = P(("parts", "seq"), "head")
    return jax.shard_map(body, mesh=mesh, in_specs=in_specs, out_specs=out_specs, check_vma=False)
```

```python
import functools

import jax
import jax.numpy as jnp
from jax import lax
from jax.experimental import pallas as pl
from jax.experimental.pallas import tpu as pltpu
from jax.sharding import PartitionSpec as P

CHUNK = 64
ROWS = 256
TILE = 256
LANES = 128
RIM = 16
SHARES = (0.4, 0.8)
GATE_SHARES = (0.6,)
HALO = 8
GROUPS = 3
FAR = 1 << 28
FLOPS_US = 1_150_000_000
bf16 = jnp.bfloat16
f32 = jnp.float32


def dot(a, b):
    return jnp.dot(a, b, preferred_element_type=f32)


def dot_nt(a, b):
    return lax.dot_general(a, b, (((1,), (1,)), ((), ())), preferred_element_type=f32)


def iota(shape, dim):
    return lax.broadcasted_iota(jnp.int32, shape, dim)


def ones_where(mask):
    return jnp.where(mask, 1.0, 0.0).astype(bf16)


def high_low(value):
    high = value.astype(bf16)
    return high, (value - high.astype(f32)).astype(bf16)


def split_lanes(value, heads):
    lane = iota(value.shape, 1)
    high = value.astype(bf16).astype(f32)
    rest = value - high
    middle = rest.astype(bf16).astype(f32)
    lowest = rest - middle
    pieces = jnp.where(lane < heads, high, jnp.where(lane < 2 * heads, middle, lowest))
    return jnp.where(lane < GROUPS * heads, pieces, 0.0).astype(bf16)


def silu(value):
    return value * jax.nn.sigmoid(value)


def call(kernel, outs, args, in_specs, out_specs, grid=(1,), scratch=(), micros=1, limit=24):
    return pl.pallas_call(
        kernel,
        grid=grid,
        in_specs=in_specs,
        out_specs=out_specs,
        out_shape=outs,
        scratch_shapes=list(scratch),
        compiler_params=pltpu.CompilerParams(vmem_limit_bytes=limit * 1024 * 1024),
        cost_estimate=pl.CostEstimate(flops=int(micros * FLOPS_US), bytes_accessed=0, transcendentals=0),
    )(*args)


def whole(array):
    rank = len(array.shape)
    return pl.BlockSpec(array.shape, lambda *_: (0,) * rank)


def columns(rows, width=TILE, start=0):
    return pl.BlockSpec((rows, width), lambda j: (0, j + start))


def smem():
    return pl.BlockSpec(memory_space=pltpu.SMEM)


def shape(*dims, dtype=bf16):
    return jax.ShapeDtypeStruct(dims, dtype)


def send_order(shards, width, quarter, place_ref, bc_ref, dt_ref, x_ref, pick_ref, *refs):
    small_refs, x_refs = refs[:shards], refs[shards:]
    rows = place_ref.shape[1]
    per = rows // shards
    heads = dt_ref.shape[0]
    both = bc_ref.shape[1]

    @pl.when(pl.program_id(0) == 0)
    def _():
        me = lax.axis_index("seq")
        place = place_ref[...]
        padded = max(8, shards)
        owner = iota((padded, rows), 0)
        first = owner * rows
        mine = (place >= first) & (place < first + rows)
        chosen = ones_where(mine)
        earlier = ones_where(iota((LANES, LANES), 0) < iota((LANES, LANES), 1))
        before, seen = [], jnp.zeros((padded, 1), f32)
        for piece in range(rows // LANES):
            part = chosen[:, piece * LANES : (piece + 1) * LANES]
            before.append(dot(part, earlier) + seen)
            seen = seen + jnp.sum(part.astype(f32), axis=1, keepdims=True)
        before = jnp.concatenate(before, 1)
        relative = jnp.where(owner >= me, owner - me, owner - me + shards)
        target = before + (relative * per).astype(f32)
        target = jnp.sum(jnp.where(mine, target, 0.0), axis=0, keepdims=True).astype(jnp.int32)
        local = jnp.sum(jnp.where(mine, (place - first + 1).astype(f32), 0.0), axis=0, keepdims=True)
        high = jnp.floor(local * (1.0 / 64.0))
        low = local - 64.0 * high
        line = iota((LANES - quarter - heads, rows), 0)
        digits = jnp.where(line == 0, high, jnp.where(line == 1, low, 0.0)).astype(bf16)
        thin = jnp.concatenate([jnp.zeros((quarter, rows), bf16), dt_ref[...], digits], 0)
        own = lax.axis_index("head") * quarter
        lane = iota((both, LANES), 1)
        taken = ones_where((iota((both, LANES), 0) == lane + own) & (lane < quarter))
        thick = dot(bc_ref[...], taken).astype(bf16)
        for k in range(shards):
            pick = ones_where(iota((per, rows), 0) + k * per == target)
            pick_ref[k * per : (k + 1) * per] = pick
            dest = jnp.where(me + k >= shards, me + k - shards, me + k)
            row = iota((RIM, rows), 0)
            rim = ones_where((row < width - 1) & (place == row + (dest * rows - (width - 1))))
            pick_ref[rows + k * RIM : rows + (k + 1) * RIM] = rim
            small_refs[k][:per] = (dot(pick, thick) + dot_nt(pick, thin)).astype(bf16)
            small_refs[k][per:] = (dot(rim, thick) + dot_nt(rim, thin)).astype(bf16)

    gather_rows(shards, True, pick_ref, x_ref, *x_refs)


def gather_rows(shards, with_rim, pick_ref, x_ref, *out_refs):
    rows = x_ref.shape[0]
    per = rows // shards
    values = x_ref[...]
    for k in range(shards):
        out_refs[k][:per] = dot(pick_ref[k * per : (k + 1) * per], values).astype(bf16)
    if with_rim:
        rims = dot(pick_ref[rows:], values).astype(bf16)
        for k in range(shards):
            out_refs[k][per:] = rims[k * RIM : (k + 1) * RIM]


def gather_parts(shards, parts, pick_ref, x_ref, *out_refs):
    rows = x_ref.shape[0]
    per = rows // shards
    values = x_ref[...]
    for number, (first, last) in enumerate(parts):

        @pl.when((pl.program_id(0) >= first) & (pl.program_id(0) < last))
        def _():
            for k in range(shards):
                taken = dot(pick_ref[k * per : (k + 1) * per], values)
                out_refs[number * shards + k][...] = taken.astype(bf16)


def distance(position, lengths, limit):
    gap, start = limit, 0
    for j in range(lengths.shape[0]):
        gap = jnp.where(position >= start, jnp.minimum(gap, position - start), gap)
        start = start + lengths[j]
    return gap


def convolve(block_of, taps, gap, width):
    total = taps[0:1] * block_of(0)
    for lag in range(1, width):
        total = total + jnp.where(gap >= lag, taps[lag : lag + 1] * block_of(lag), 0.0)
    return silu(total).astype(bf16)


def prepare(
    shards, groups, width, heads, head_dim, lengths, first_ref, taps_ref, lines_ref, *refs
):
    (
        pick_ref, rims_ref, gap_ref, score_high_ref, score_low_ref, query_ref, kept_query_ref,
        keys_ref, inside_ref, outside_ref, carried_ref, expand_ref, factor_ref, rest_ref,
        packed, log_sums, steps,
    ) = refs[-17:]
    others = refs[:-17]
    rows = pick_ref.shape[0]
    per = rows // shards
    group = per + RIM
    state = query_ref.shape[1]
    base = lax.axis_index("seq") * rows
    sources = [first_ref]
    flips = [0]
    for ref in others:
        flips = flips + [flip ^ (groups // (2 * len(flips))) for flip in flips]
        sources = sources + [ref.at[n * shards * group : (n + 1) * shards * group] for n in range(len(sources))]
    quarter = 2 * state // len(sources)

    def main(ref):
        return jnp.concatenate([ref[k * group : k * group + per] for k in range(shards)], 0)

    def rim(ref):
        return jnp.concatenate([ref[k * group + per : (k + 1) * group] for k in range(shards)], 0)

    own_main = main(first_ref)
    lane = iota((8, LANES), 1)
    high_lane = quarter + heads
    weights = jnp.where(lane == high_lane, 64.0, jnp.where(lane == high_lane + 1, 1.0, 0.0)).astype(bf16)
    slots = dot_nt(weights, own_main)[0:1].astype(jnp.int32) - 1
    rim_slots = dot_nt(weights, rim(first_ref))[0:1].astype(jnp.int32) - 1 - rows + HALO
    rim_pick = ones_where(iota((RIM, shards * RIM), 0) == rim_slots)
    rims_ref[...] = rim_pick
    me = lax.axis_index("head")
    bc_main, bc_rim = 0.0, 0.0
    for flip, ref in zip(flips, sources):
        lane = iota((LANES, 2 * state), 0)
        spread = ones_where((lane < quarter) & (lane + (me ^ flip) * quarter == iota((LANES, 2 * state), 1)))
        bc_main = bc_main + dot(main(ref), spread)
        bc_rim = bc_rim + dot(rim(ref), spread)
    bc_main = bc_main.astype(bf16)
    packed[0:HALO] = dot(rim_pick, bc_rim.astype(bf16))[0:HALO]
    lane_of = iota((LANES, LANES), 0) - quarter
    wide = iota((LANES, LANES), 1)
    copy_dt = ones_where(
        (lane_of >= 0) & (lane_of < heads)
        & ((lane_of == wide) | (lane_of + heads == wide) | (lane_of + 2 * heads == wide))
    )
    decay_rate = -jnp.exp(lines_ref[1:2])
    row_in = iota((ROWS, ROWS), 0)
    col_in = iota((ROWS, ROWS), 1)
    same_chunk = (row_in // CHUNK) == (col_in // CHUNK)
    lower = same_chunk & (col_in <= row_in)
    sums = ones_where(lower)
    expand = iota((LANES, heads * head_dim), 0)
    head_of = jnp.where(expand >= 2 * heads, expand - 2 * heads, jnp.where(expand >= heads, expand - heads, expand))
    channel = iota((LANES, heads * head_dim), 1)
    expand = ones_where(
        (expand < GROUPS * heads) & (channel >= head_of * head_dim) & (channel < (head_of + 1) * head_dim)
    )
    expand_ref[...] = expand
    for b in range(rows // ROWS):
        here = slice(b * ROWS, (b + 1) * ROWS)
        pick = ones_where(iota((ROWS, rows), 0) + b * ROWS == slots)
        pick_ref[here] = pick
        packed[HALO + b * ROWS : HALO + (b + 1) * ROWS] = dot(pick, bc_main)
        raw = dot(pick, own_main).astype(bf16)
        step = jax.nn.softplus(dot(raw, copy_dt) + lines_ref[0:1])
        log_decay = decay_rate * step
        high = log_decay.astype(bf16)
        rest = log_decay - high.astype(f32)
        middle = rest.astype(bf16)
        lowest = (rest - middle.astype(f32)).astype(bf16)
        log_sums[here] = dot(sums, high) + dot(sums, middle) + dot(sums, lowest)
        steps[here] = step
    total = jnp.zeros((1, LANES), f32)
    chunks = rows // CHUNK
    factors = []
    pending = None
    for c in range(chunks):
        here = slice(c * CHUNK, (c + 1) * CHUNK)
        logs = log_sums[here]
        centre = logs[CHUNK // 2 - 1 : CHUNK // 2]
        last = logs[CHUNK - 1 : CHUNK]
        outside_ref[here] = split_lanes(jnp.exp(logs - centre), heads)
        inside_ref[here] = split_lanes(jnp.exp(centre - logs) * steps[here], heads)
        offset = iota((CHUNK, LANES), 0) + c * CHUNK
        gap = distance(offset + base, lengths, FAR)
        gap_ref[here] = gap
        carried_ref[here] = split_lanes(jnp.where(gap > offset, jnp.exp(logs + total), 0.0), heads)
        if pending is not None:
            factors.append(jnp.exp(pending + centre))
        pending = last - centre
        total = total + last
    factors.append(jnp.exp(pending))
    end_gap = distance(base + rows - 1, lengths, FAR)
    decay = jnp.where(end_gap >= rows, jnp.exp(total), 0.0)
    for c in range(chunks):
        log_sums[c : c + 1] = factors[c]
    factor_ref[...] = dot(split_lanes(log_sums[0:chunks], heads), expand)
    log_sums[0:1] = decay
    log_sums[1:2] = lines_ref[2:3]
    rest_ref[...] = dot(split_lanes(log_sums[0:8], heads), expand)
    for b in range(rows // ROWS):
        here = slice(b * ROWS, (b + 1) * ROWS)
        gap = gap_ref[here]
        wide_gap = jnp.concatenate([gap] * (2 * state // LANES), 1)

        def shifted(lag):
            return packed[HALO + b * ROWS - lag : HALO + (b + 1) * ROWS - lag]

        both = convolve(shifted, taps_ref[...], wide_gap, width)
        keys, queries = both[:, :state], both[:, state:]
        query_ref[here] = queries
        offset = iota((ROWS, state), 0)
        in_chunk = offset % CHUNK
        zero = jnp.zeros_like(queries)
        kept_query_ref[here] = jnp.where(gap > in_chunk, queries.astype(f32), 0.0).astype(bf16)
        ends = jnp.zeros((ROWS, state), jnp.int32)
        for c in range(ROWS // CHUNK):
            end = base + b * ROWS + (c + 1) * CHUNK - 1
            ends = jnp.where(offset // CHUNK == c, distance(end, lengths, FAR), ends)
        last_keys = jnp.where(CHUNK - 1 - in_chunk <= ends, keys.astype(f32), 0.0)
        keys_ref[:, here] = last_keys.T.astype(bf16)
        scores = dot_nt(queries, keys)
        gap_square = jnp.concatenate([gap] * (ROWS // LANES), 1)
        scores = jnp.where(lower & (row_in - col_in <= gap_square), scores, 0.0)
        high, low = high_low(scores)
        score_high_ref[here] = high
        score_low_ref[here] = low


def scan_columns(
    shards, width,
    lengths, pick_ref, rims_ref, gap_ref, score_high_ref, score_low_ref, kept_query_ref, keys_ref,
    inside_ref, outside_ref, expand_ref, factor_ref, rest_ref, taps_ref, *refs,
):
    blocks = refs[:shards]
    out_ref, state_ref, arrived, packed = refs[shards:]
    rows = pick_ref.shape[0]
    per = rows // shards
    base = lax.axis_index("seq") * rows
    for k in range(shards):
        arrived[k * per : (k + 1) * per] = blocks[k][:per]
    rim = jnp.concatenate([blocks[k][per:] for k in range(shards)], 0)
    packed[0:HALO] = dot(rims_ref[...], rim)[0:HALO]
    expand = expand_ref[...]
    state_ref[...] = jnp.zeros_like(state_ref)
    for b in range(rows // ROWS):
        here = slice(b * ROWS, (b + 1) * ROWS)
        packed[HALO + b * ROWS : HALO + (b + 1) * ROWS] = dot(pick_ref[here], arrived[...])
        gap = gap_ref[here]

        def shifted(lag):
            return packed[HALO + b * ROWS - lag : HALO + (b + 1) * ROWS - lag]

        conv = convolve(shifted, taps_ref[...], jnp.concatenate([gap] * (TILE // LANES), 1), width).astype(f32)
        scaled = conv * dot(inside_ref[here], expand)
        high, low = high_low(scaled)
        score_high, score_low = score_high_ref[here], score_low_ref[here]
        total = dot(score_high, high) + dot(score_low, high) + dot(score_high, low)
        outside = dot(outside_ref[here], expand)
        carry = state_ref[...]
        parts = []
        for c in range(ROWS // CHUNK):
            inner = slice(c * CHUNK, (c + 1) * CHUNK)
            place = slice(b * ROWS + c * CHUNK, b * ROWS + (c + 1) * CHUNK)
            carry_high, carry_low = high_low(carry)
            kept = kept_query_ref[place]
            parts.append(dot(kept, carry_high) + dot(kept, carry_low))
            keys = keys_ref[:, place]
            added = dot(keys, high[inner]) + dot(keys, low[inner])
            end = base + b * ROWS + (c + 1) * CHUNK - 1
            keep = jnp.where(distance(end, lengths, FAR) >= CHUNK, 1.0, 0.0)
            number = b * (ROWS // CHUNK) + c
            carry = (carry * keep + added) * factor_ref[number : number + 1]
        state_ref[...] = carry
        out_ref[here] = outside * (total + jnp.concatenate(parts, 0)) + rest_ref[1:2] * conv


def gate_columns(shards, pick_ref, query_ref, carried_ref, expand_ref, scan_ref, state_ref, *refs):
    blocks = refs[:shards]
    out_ref, total_ref, arrived, square_ref = refs[shards:]
    rows = pick_ref.shape[0]
    per = rows // shards
    for k in range(shards):
        arrived[k * per : (k + 1) * per] = blocks[k][...]

    @pl.when(pl.program_id(0) == 0)
    def _():
        square_ref[...] = jnp.zeros_like(square_ref)

    carry_high, carry_low = high_low(state_ref[...])
    for b in range(rows // ROWS):
        here = slice(b * ROWS, (b + 1) * ROWS)
        gate = dot(pick_ref[here], arrived[...])
        queries = query_ref[here]
        earlier = dot(queries, carry_high) + dot(queries, carry_low)
        outputs = scan_ref[here] + dot(carried_ref[here], expand_ref[...]) * earlier
        gated = outputs * silu(gate)
        out_ref[here] = gated
        squares = gated * gated
        part = squares[:, :LANES]
        for piece in range(1, TILE // LANES):
            part = part + squares[:, piece * LANES : (piece + 1) * LANES]
        square_ref[here] = square_ref[here] + part

    @pl.when(pl.program_id(0) == pl.num_programs(0) - 1)
    def _():
        for b in range(rows // ROWS):
            here = slice(b * ROWS, (b + 1) * ROWS)
            total_ref[:, here] = jnp.sum(square_ref[here].T, axis=0, keepdims=True)


def normalize(count, total_ref, gain_ref, *refs):
    pieces, out_ref = refs[:-1], refs[-1]
    scale = lax.rsqrt(total_ref[...] / count + 1e-05)
    scale = jnp.broadcast_to(scale, (LANES, scale.shape[1])).T
    first = 0
    for ref in pieces:
        for tile in range(ref.shape[1] // LANES):
            here = slice(first + tile * LANES, first + (tile + 1) * LANES)
            value = ref[:, tile * LANES : (tile + 1) * LANES] * scale * gain_ref[:, here]
            out_ref[:, here] = value.astype(bf16)
        first += ref.shape[1]


def moved(block, axis, steps):
    count = lax.axis_size(axis)
    return lax.ppermute(block, axis, [(i, (i + steps) % count) for i in range(count)])


def after(value, *others):
    return lax.optimization_barrier((value, *others))[0]


def cut(tiles, shares):
    cuts = sorted({0, *(round(tiles * share) for share in shares), tiles})
    return list(zip(cuts, cuts[1:]))


def body(xs, gate_in, bc_in, dt_in, placement, lengths, conv_x, conv_bc, a_log, dt_bias, d_skip, norm_gain):
    shards = lax.axis_size("seq")
    groups = lax.axis_size("head")
    rows, inner = xs.shape
    width = conv_x.shape[0]
    heads = a_log.shape[0]
    head_dim = inner // heads
    state = bc_in.shape[1] // 2
    per = rows // shards
    group = per + RIM
    tiles = inner // TILE
    chunks = rows // CHUNK
    parts = cut(tiles, SHARES)
    gate_parts = cut(tiles, GATE_SHARES)
    triple = jnp.stack([dt_bias, a_log, d_skip])
    lines = jnp.pad(jnp.concatenate([triple] * GROUPS, 1), ((0, 5), (0, LANES - GROUPS * heads)))

    place = placement.reshape(1, rows)
    thin = dt_in.T
    full = rows + shards * RIM
    quarter = 2 * state // groups
    first, last = parts[0]
    sent = call(
        functools.partial(send_order, shards, width, quarter),
        [shape(full, rows)] + [shape(group, LANES)] * shards + [shape(group, (last - first) * TILE)] * shards,
        (place, bc_in, thin, xs),
        [whole(place), whole(bc_in), whole(thin), columns(rows)],
        [whole(shape(full, rows))] + [whole(shape(group, LANES))] * shards + [columns(group)] * shards,
        grid=(last - first,),
        micros=7,
        limit=56,
    )
    picks, small, x_send = sent[0], sent[1 : 1 + shards], [sent[1 + shards :]]
    small = [small[0]] + [moved(small[k], "seq", k) for k in range(1, shards)]
    arrived = [[x_send[0][0]] + [moved(x_send[0][k], "seq", k) for k in range(1, shards)]]

    small = [jnp.concatenate(small, 0)]
    mask = groups // 2
    while mask:
        held = jnp.concatenate(small, 0) if len(small) > 1 else small[0]
        small.append(lax.ppermute(held, "head", [(i, i ^ mask) for i in range(groups)]))
        mask //= 2
    for first, last in parts[1:]:
        x_send.append(
            call(
                functools.partial(gather_rows, shards, True),
                [shape(group, (last - first) * TILE)] * shards,
                (picks, xs),
                [whole(picks), columns(rows, start=first)],
                [columns(group)] * shards,
                grid=(last - first,),
                micros=2 * (last - first),
            )
        )
    def within(first, last):
        return pl.BlockSpec((per, TILE), lambda j: (0, jnp.clip(j - first, 0, last - first - 1)))

    gate_send = call(
        functools.partial(gather_parts, shards, gate_parts),
        [shape(per, (last - first) * TILE) for first, last in gate_parts for _ in range(shards)],
        (picks, gate_in),
        [whole(shape(rows, rows)), columns(rows)],
        [within(first, last) for first, last in gate_parts for _ in range(shards)],
        grid=(tiles,),
        micros=2 * tiles,
    )
    gate_send = [gate_send[number * shards : (number + 1) * shards] for number in range(len(gate_parts))]

    kept = [
        shape(rows, rows),
        shape(RIM, shards * RIM),
        shape(rows, LANES, dtype=jnp.int32),
        shape(rows, ROWS),
        shape(rows, ROWS),
        shape(rows, state),
        shape(rows, state),
        shape(state, rows),
        shape(rows, LANES),
        shape(rows, LANES),
        shape(rows, LANES),
        shape(LANES, inner),
        shape(chunks, inner, dtype=f32),
        shape(8, inner, dtype=f32),
    ]
    (
        pick, rims, gap, score_high, score_low, query, kept_query,
        keys, inside, outside, carried, expand, factor, rest,
    ) = call(
        functools.partial(prepare, shards, groups, width, heads, head_dim),
        kept,
        (lengths, small[0], conv_bc, lines, *small[1:]),
        [smem()] + [whole(s) for s in (small[0], conv_bc, lines, *small[1:])],
        [whole(s) for s in kept],
        scratch=[
            pltpu.VMEM((rows + HALO, 2 * state), f32),
            pltpu.VMEM((rows, LANES), f32),
            pltpu.VMEM((rows, LANES), f32),
        ],
        micros=8,
    )

    def stream(send, before, *others):
        return [send[0]] + [
            moved(after(send[k], before[k], *others), "seq", k) for k in range(1, shards)
        ]

    if len(parts) > 1:
        arrived.append(stream(x_send[1], arrived[0], rims, gate_send[0][0], x_send[-1][0]))

    scans, ends, states, gates = [], [], [], []
    for number, part in enumerate(parts):
        blocks = arrived[number]
        first, last = part
        size = (last - first) * TILE
        if ends:
            blocks = [after(blocks[0], ends[-1])] + blocks[1:]
        scanned, local_state = call(
            functools.partial(scan_columns, shards, width),
            [shape(rows, size, dtype=f32), shape(state, size, dtype=f32)],
            (
                lengths, pick, rims, gap, score_high, score_low, kept_query, keys, inside, outside,
                expand, factor, rest, conv_x, *blocks,
            ),
            [smem()]
            + [whole(a) for a in (pick, rims, gap, score_high, score_low, kept_query, keys, inside, outside)]
            + [columns(n, start=first) for n in (LANES, chunks, 8, width)]
            + [columns(group)] * shards,
            [columns(rows), columns(state)],
            grid=(last - first,),
            scratch=[pltpu.VMEM((rows, TILE), bf16), pltpu.VMEM((rows + HALO, TILE), f32)],
            micros=5 * (last - first),
        )
        scans.append(scanned)
        ends.append(local_state)
        if number + 2 < len(parts):
            arrived.append(stream(x_send[number + 2], arrived[number + 1], local_state))
        if not gates and number + 2 >= len(parts):
            gates.append(stream(gate_send[0], arrived[-1], local_state))
            for send in gate_send[1:]:
                gates.append(stream(send, gates[-1]))
        following = (arrived + gates)[number + 1]
        incoming = leaving = None
        for step in range(1, shards):
            leaving = after(local_state, following[1])
            if incoming is not None:
                leaving = leaving + rest[0:1, first * TILE : last * TILE] * incoming
            received = lax.ppermute(leaving, "seq", [(step - 1, step)])
            incoming = received if incoming is None else incoming + received
        states.append(incoming)

    outs, totals = [], []
    for tile in range(tiles):
        part = sum(tile >= last for _, last in parts)
        gate_part = sum(tile >= last for _, last in gate_parts)
        blocks = gates[gate_part]
        if gate_part + 1 < len(gates):
            blocks = [after(blocks[0], gates[gate_part + 1][1])] + blocks[1:]
        gated, total = call(
            functools.partial(gate_columns, shards),
            [shape(rows, TILE, dtype=f32), shape(1, rows, dtype=f32)],
            (pick, query, carried, expand, scans[part], states[part], *blocks),
            [whole(pick), whole(query), whole(carried), columns(LANES, start=tile)]
            + [columns(n, start=tile - parts[part][0]) for n in (rows, state)]
            + [columns(per, start=tile - gate_parts[gate_part][0])] * shards,
            [columns(rows), whole(shape(1, rows))],
            scratch=[pltpu.VMEM((rows, TILE), bf16), pltpu.VMEM((rows, LANES), f32)],
            micros=3,
        )
        outs.append(gated)
        totals.append(total)
    total = lax.psum(sum(totals), "head")
    gain = norm_gain.reshape(1, inner)
    return call(
        functools.partial(normalize, inner * groups),
        shape(rows, inner),
        (total, gain, *outs),
        [pl.BlockSpec((1, ROWS), lambda i: (0, i)), whole(gain)]
        + [pl.BlockSpec((ROWS, out.shape[1]), lambda i: (i, 0)) for out in outs],
        pl.BlockSpec((ROWS, inner), lambda i: (i, 0)),
        grid=(rows // ROWS,),
        micros=5,
    )


def solution(mesh):
    in_specs = (
        P(("parts", "seq"), "head"),
        P(("parts", "seq"), "head"),
        P(("parts", "seq"), None),
        P(("parts", "seq"), "head"),
        P(("parts", "seq")),
        P("parts"),
        P(None, "head"),
        P(),
        P("head"),
        P("head"),
        P("head"),
        P("head"),
    )
    out_specs = P(("parts", "seq"), "head")
    return jax.shard_map(body, mesh=mesh, in_specs=in_specs, out_specs=out_specs, check_vma=False)
```

```python
import functools

import jax
import jax.numpy as jnp
from jax import lax
from jax.experimental import pallas as pl
from jax.experimental.pallas import tpu as pltpu
from jax.sharding import PartitionSpec as P

CHUNK = 64
ROWS = 256
TILE = 256
LANES = 128
RIM = 16
SHARES = (0.4,)
GATE_SHARES = (0.6,)
WINDOW = 2
TINY = 2.0**-100
HALO = 8
GROUPS = 3
FAR = 1 << 28
FLOPS_US = 1_150_000_000
bf16 = jnp.bfloat16
f32 = jnp.float32


def dot(a, b):
    return jnp.dot(a, b, preferred_element_type=f32)


def dot_nt(a, b):
    return lax.dot_general(a, b, (((1,), (1,)), ((), ())), preferred_element_type=f32)


def iota(shape, dim):
    return lax.broadcasted_iota(jnp.int32, shape, dim)


def ones_where(mask):
    return jnp.where(mask, 1.0, 0.0).astype(bf16)


def high_low(value):
    high = value.astype(bf16)
    return high, (value - high.astype(f32)).astype(bf16)


def split_lanes(value, heads):
    lane = iota(value.shape, 1)
    high = value.astype(bf16).astype(f32)
    rest = value - high
    middle = rest.astype(bf16).astype(f32)
    lowest = rest - middle
    pieces = jnp.where(lane < heads, high, jnp.where(lane < 2 * heads, middle, lowest))
    return jnp.where(lane < GROUPS * heads, pieces, 0.0).astype(bf16)


def silu(value):
    return value * jax.nn.sigmoid(value)


def call(kernel, outs, args, in_specs, out_specs, grid=(1,), scratch=(), micros=1, limit=24):
    return pl.pallas_call(
        kernel,
        grid=grid,
        in_specs=in_specs,
        out_specs=out_specs,
        out_shape=outs,
        scratch_shapes=list(scratch),
        compiler_params=pltpu.CompilerParams(vmem_limit_bytes=limit * 1024 * 1024),
        cost_estimate=pl.CostEstimate(flops=int(micros * FLOPS_US), bytes_accessed=0, transcendentals=0),
    )(*args)


def whole(array):
    rank = len(array.shape)
    return pl.BlockSpec(array.shape, lambda *_: (0,) * rank)


def columns(rows, width=TILE, start=0):
    return pl.BlockSpec((rows, width), lambda j: (0, j + start))


def smem():
    return pl.BlockSpec(memory_space=pltpu.SMEM)


def shape(*dims, dtype=bf16):
    return jax.ShapeDtypeStruct(dims, dtype)


def send_order(shards, width, quarter, place_ref, bc_ref, dt_ref, x_ref, pick_ref, *refs):
    small_refs, x_refs = refs[:shards], refs[shards:]
    rows = place_ref.shape[1]
    per = rows // shards
    heads = dt_ref.shape[0]
    both = bc_ref.shape[1]

    @pl.when(pl.program_id(0) == 0)
    def _():
        me = lax.axis_index("seq")
        place = place_ref[...]
        padded = max(8, shards)
        owner = iota((padded, rows), 0)
        first = owner * rows
        mine = (place >= first) & (place < first + rows)
        chosen = ones_where(mine)
        earlier = ones_where(iota((LANES, LANES), 0) < iota((LANES, LANES), 1))
        before, seen = [], jnp.zeros((padded, 1), f32)
        for piece in range(rows // LANES):
            part = chosen[:, piece * LANES : (piece + 1) * LANES]
            before.append(dot(part, earlier) + seen)
            seen = seen + jnp.sum(part.astype(f32), axis=1, keepdims=True)
        before = jnp.concatenate(before, 1)
        relative = jnp.where(owner >= me, owner - me, owner - me + shards)
        target = before + (relative * per).astype(f32)
        target = jnp.sum(jnp.where(mine, target, 0.0), axis=0, keepdims=True).astype(jnp.int32)
        local = jnp.sum(jnp.where(mine, (place - first + 1).astype(f32), 0.0), axis=0, keepdims=True)
        high = jnp.floor(local * (1.0 / 64.0))
        low = local - 64.0 * high
        line = iota((LANES - quarter - heads, rows), 0)
        digits = jnp.where(line == 0, high, jnp.where(line == 1, low, 0.0)).astype(bf16)
        thin = jnp.concatenate([jnp.zeros((quarter, rows), bf16), dt_ref[...], digits], 0)
        own = lax.axis_index("head") * quarter
        lane = iota((both, LANES), 1)
        taken = ones_where((iota((both, LANES), 0) == lane + own) & (lane < quarter))
        thick = dot(bc_ref[...], taken).astype(bf16)
        for k in range(shards):
            pick = ones_where(iota((per, rows), 0) + k * per == target)
            pick_ref[k * per : (k + 1) * per] = pick
            dest = jnp.where(me + k >= shards, me + k - shards, me + k)
            row = iota((RIM, rows), 0)
            rim = ones_where((row < width - 1) & (place == row + (dest * rows - (width - 1))))
            pick_ref[rows + k * RIM : rows + (k + 1) * RIM] = rim
            small_refs[k][:per] = (dot(pick, thick) + dot_nt(pick, thin)).astype(bf16)
            small_refs[k][per:] = (dot(rim, thick) + dot_nt(rim, thin)).astype(bf16)

    gather_rows(shards, True, pick_ref, x_ref, *x_refs)


def gather_rows(shards, with_rim, pick_ref, x_ref, *out_refs):
    rows = x_ref.shape[0]
    per = rows // shards
    values = x_ref[...]
    for k in range(shards):
        out_refs[k][:per] = dot(pick_ref[k * per : (k + 1) * per], values).astype(bf16)
    if with_rim:
        rims = dot(pick_ref[rows:], values).astype(bf16)
        for k in range(shards):
            out_refs[k][per:] = rims[k * RIM : (k + 1) * RIM]


def gather_parts(shards, parts, pick_ref, x_ref, *out_refs):
    rows = x_ref.shape[0]
    per = rows // shards
    values = x_ref[...]
    for number, (first, last) in enumerate(parts):

        @pl.when((pl.program_id(0) >= first) & (pl.program_id(0) < last))
        def _():
            for k in range(shards):
                taken = dot(pick_ref[k * per : (k + 1) * per], values)
                out_refs[number * shards + k][...] = taken.astype(bf16)


def distance(position, lengths, limit):
    gap, start = limit, 0
    for j in range(lengths.shape[0]):
        gap = jnp.where(position >= start, jnp.minimum(gap, position - start), gap)
        start = start + lengths[j]
    return gap


def convolve(block_of, taps, gap, width):
    total = taps[0:1] * block_of(0)
    for lag in range(1, width):
        total = total + jnp.where(gap >= lag, taps[lag : lag + 1] * block_of(lag), 0.0)
    return silu(total).astype(bf16)


def prepare(
    shards, groups, width, heads, head_dim, lengths, first_ref, taps_ref, lines_ref, *refs
):
    (
        pick_ref, rims_ref, gap_ref, score_high_ref, score_low_ref, query_ref, kept_query_ref,
        keys_ref, inside_ref, outside_ref, carried_ref, expand_ref, factor_ref, rest_ref,
        packed, log_sums, steps,
    ) = refs[-17:]
    others = refs[:-17]
    rows = pick_ref.shape[0]
    per = rows // shards
    group = per + RIM
    state = query_ref.shape[1]
    base = lax.axis_index("seq") * rows
    sources = [first_ref]
    flips = [0]
    for ref in others:
        flips = flips + [flip ^ (groups // (2 * len(flips))) for flip in flips]
        sources = sources + [ref.at[n * shards * group : (n + 1) * shards * group] for n in range(len(sources))]
    quarter = 2 * state // len(sources)

    def main(ref):
        return jnp.concatenate([ref[k * group : k * group + per] for k in range(shards)], 0)

    def rim(ref):
        return jnp.concatenate([ref[k * group + per : (k + 1) * group] for k in range(shards)], 0)

    own_main = main(first_ref)
    lane = iota((8, LANES), 1)
    high_lane = quarter + heads
    weights = jnp.where(lane == high_lane, 64.0, jnp.where(lane == high_lane + 1, 1.0, 0.0)).astype(bf16)
    slots = dot_nt(weights, own_main)[0:1].astype(jnp.int32) - 1
    rim_slots = dot_nt(weights, rim(first_ref))[0:1].astype(jnp.int32) - 1 - rows + HALO
    rim_pick = ones_where(iota((RIM, shards * RIM), 0) == rim_slots)
    rims_ref[...] = rim_pick
    me = lax.axis_index("head")
    bc_main, bc_rim = 0.0, 0.0
    for flip, ref in zip(flips, sources):
        lane = iota((LANES, 2 * state), 0)
        spread = ones_where((lane < quarter) & (lane + (me ^ flip) * quarter == iota((LANES, 2 * state), 1)))
        bc_main = bc_main + dot(main(ref), spread)
        bc_rim = bc_rim + dot(rim(ref), spread)
    bc_main = bc_main.astype(bf16)
    packed[0:HALO] = dot(rim_pick, bc_rim.astype(bf16))[0:HALO]
    lane_of = iota((LANES, LANES), 0) - quarter
    wide = iota((LANES, LANES), 1)
    copy_dt = ones_where(
        (lane_of >= 0) & (lane_of < heads)
        & ((lane_of == wide) | (lane_of + heads == wide) | (lane_of + 2 * heads == wide))
    )
    decay_rate = -jnp.exp(lines_ref[1:2])
    row_in = iota((ROWS, ROWS), 0)
    col_in = iota((ROWS, ROWS), 1)
    same_chunk = (row_in // CHUNK) == (col_in // CHUNK)
    lower = same_chunk & (col_in <= row_in)
    sums = ones_where(lower)
    expand = iota((LANES, heads * head_dim), 0)
    head_of = jnp.where(expand >= 2 * heads, expand - 2 * heads, jnp.where(expand >= heads, expand - heads, expand))
    channel = iota((LANES, heads * head_dim), 1)
    expand = ones_where(
        (expand < GROUPS * heads) & (channel >= head_of * head_dim) & (channel < (head_of + 1) * head_dim)
    )
    expand_ref[...] = expand
    for b in range(rows // ROWS):
        here = slice(b * ROWS, (b + 1) * ROWS)
        pick = ones_where(iota((ROWS, rows), 0) + b * ROWS == slots)
        pick_ref[here] = pick
        packed[HALO + b * ROWS : HALO + (b + 1) * ROWS] = dot(pick, bc_main)
        raw = dot(pick, own_main).astype(bf16)
        step = jax.nn.softplus(dot(raw, copy_dt) + lines_ref[0:1])
        log_decay = decay_rate * step
        high = log_decay.astype(bf16)
        rest = log_decay - high.astype(f32)
        middle = rest.astype(bf16)
        lowest = (rest - middle.astype(f32)).astype(bf16)
        log_sums[here] = dot(sums, high) + dot(sums, middle) + dot(sums, lowest)
        steps[here] = step
    total = jnp.zeros((1, LANES), f32)
    chunks = rows // CHUNK
    factors = []
    pending = None
    for c in range(chunks):
        here = slice(c * CHUNK, (c + 1) * CHUNK)
        logs = log_sums[here]
        centre = logs[CHUNK // 2 - 1 : CHUNK // 2]
        last = logs[CHUNK - 1 : CHUNK]
        outside_ref[here] = split_lanes(jnp.exp(logs - centre), heads)
        inside_ref[here] = split_lanes(jnp.exp(centre - logs) * steps[here], heads)
        offset = iota((CHUNK, LANES), 0) + c * CHUNK
        gap = distance(offset + base, lengths, FAR)
        gap_ref[here] = gap
        carried_ref[here] = split_lanes(jnp.where(gap > offset, jnp.exp(logs + total), 0.0), heads)
        if pending is not None:
            factors.append(jnp.exp(pending + centre))
        pending = last - centre
        total = total + last
    factors.append(jnp.exp(pending))
    end_gap = distance(base + rows - 1, lengths, FAR)
    decay = jnp.where(end_gap >= rows, jnp.exp(total), 0.0)
    for c in range(chunks):
        log_sums[c : c + 1] = factors[c]
    factor_ref[...] = dot(split_lanes(log_sums[0:chunks], heads), expand)
    log_sums[0:1] = decay
    log_sums[1:2] = lines_ref[2:3]
    rest_ref[...] = dot(split_lanes(log_sums[0:8], heads), expand)
    for b in range(rows // ROWS):
        here = slice(b * ROWS, (b + 1) * ROWS)
        gap = gap_ref[here]
        wide_gap = jnp.concatenate([gap] * (2 * state // LANES), 1)

        def shifted(lag):
            return packed[HALO + b * ROWS - lag : HALO + (b + 1) * ROWS - lag]

        both = convolve(shifted, taps_ref[...], wide_gap, width)
        keys, queries = both[:, :state], both[:, state:]
        query_ref[here] = queries
        offset = iota((ROWS, state), 0)
        in_chunk = offset % CHUNK
        zero = jnp.zeros_like(queries)
        kept_query_ref[here] = jnp.where(gap > in_chunk, queries.astype(f32), 0.0).astype(bf16)
        ends = jnp.zeros((ROWS, state), jnp.int32)
        for c in range(ROWS // CHUNK):
            end = base + b * ROWS + (c + 1) * CHUNK - 1
            ends = jnp.where(offset // CHUNK == c, distance(end, lengths, FAR), ends)
        last_keys = jnp.where(CHUNK - 1 - in_chunk <= ends, keys.astype(f32), 0.0)
        keys_ref[:, here] = last_keys.T.astype(bf16)
        scores = dot_nt(queries, keys)
        gap_square = jnp.concatenate([gap] * (ROWS // LANES), 1)
        scores = jnp.where(lower & (row_in - col_in <= gap_square), scores, 0.0)
        high, low = high_low(scores)
        score_high_ref[here] = high
        score_low_ref[here] = low


def scan_columns(
    shards, width,
    lengths, pick_ref, rims_ref, gap_ref, score_high_ref, score_low_ref, kept_query_ref, keys_ref,
    inside_ref, outside_ref, expand_ref, factor_ref, rest_ref, taps_ref, *refs,
):
    blocks = refs[:shards]
    out_ref, state_ref, size_ref, arrived, packed = refs[shards:]
    rows = pick_ref.shape[0]
    per = rows // shards
    base = lax.axis_index("seq") * rows
    for k in range(shards):
        arrived[k * per : (k + 1) * per] = blocks[k][:per]
    rim = jnp.concatenate([blocks[k][per:] for k in range(shards)], 0)
    packed[0:HALO] = dot(rims_ref[...], rim)[0:HALO]
    expand = expand_ref[...]
    state_ref[...] = jnp.zeros_like(state_ref)
    for b in range(rows // ROWS):
        here = slice(b * ROWS, (b + 1) * ROWS)
        packed[HALO + b * ROWS : HALO + (b + 1) * ROWS] = dot(pick_ref[here], arrived[...])
        gap = gap_ref[here]

        def shifted(lag):
            return packed[HALO + b * ROWS - lag : HALO + (b + 1) * ROWS - lag]

        conv = convolve(shifted, taps_ref[...], jnp.concatenate([gap] * (TILE // LANES), 1), width).astype(f32)
        scaled = conv * dot(inside_ref[here], expand)
        high, low = high_low(scaled)
        score_high, score_low = score_high_ref[here], score_low_ref[here]
        total = dot(score_high, high) + dot(score_low, high) + dot(score_high, low)
        outside = dot(outside_ref[here], expand)
        carry = state_ref[...]
        parts = []
        for c in range(ROWS // CHUNK):
            inner = slice(c * CHUNK, (c + 1) * CHUNK)
            place = slice(b * ROWS + c * CHUNK, b * ROWS + (c + 1) * CHUNK)
            carry_high, carry_low = high_low(carry)
            kept = kept_query_ref[place]
            parts.append(dot(kept, carry_high) + dot(kept, carry_low))
            keys = keys_ref[:, place]
            added = dot(keys, high[inner]) + dot(keys, low[inner])
            end = base + b * ROWS + (c + 1) * CHUNK - 1
            keep = jnp.where(distance(end, lengths, FAR) >= CHUNK, 1.0, 0.0)
            number = b * (ROWS // CHUNK) + c
            carry = (carry * keep + added) * factor_ref[number : number + 1]
        state_ref[...] = carry
        out_ref[here] = outside * (total + jnp.concatenate(parts, 0)) + rest_ref[1:2] * conv
    largest = jnp.max(jnp.abs(state_ref[...]), axis=0, keepdims=True)
    size_ref[...] = jnp.broadcast_to(jnp.maximum(largest, TINY), size_ref.shape)


def gate_columns(shards, sum_ref, pick_ref, query_ref, carried_ref, expand_ref, scan_ref, state_ref, *refs):
    blocks = refs[:shards]
    out_ref, total_ref, arrived, square_ref = refs[shards:]
    rows = pick_ref.shape[0]
    per = rows // shards
    for k in range(shards):
        arrived[k * per : (k + 1) * per] = blocks[k][...]

    @pl.when(pl.program_id(0) == 0)
    def _():
        square_ref[...] = jnp.zeros_like(square_ref)

    carry_high, carry_low = high_low(state_ref[...])
    for b in range(rows // ROWS):
        here = slice(b * ROWS, (b + 1) * ROWS)
        gate = dot(pick_ref[here], arrived[...])
        queries = query_ref[here]
        earlier = dot(queries, carry_high) + dot(queries, carry_low)
        outputs = scan_ref[here] + dot(carried_ref[here], expand_ref[...]) * earlier
        gated = outputs * silu(gate)
        out_ref[here] = gated
        squares = gated * gated
        part = squares[:, :LANES]
        for piece in range(1, TILE // LANES):
            part = part + squares[:, piece * LANES : (piece + 1) * LANES]
        square_ref[here] = square_ref[here] + part

    @pl.when(pl.program_id(0) == pl.num_programs(0) - 1)
    def _():
        for b in range(rows // ROWS):
            here = slice(b * ROWS, (b + 1) * ROWS)
            total_ref[:, here] = sum_ref[:, here] + jnp.sum(square_ref[here].T, axis=0, keepdims=True)


def normalize(count, groups, *refs):
    pieces, out_ref = refs[groups + 1 : -1], refs[-1]
    gain_ref = refs[groups]
    scale = refs[0][...]
    for ref in refs[1:groups]:
        scale = scale + ref[...]
    scale = lax.rsqrt(scale / count + 1e-05)
    scale = jnp.broadcast_to(scale, (LANES, scale.shape[1])).T
    first = 0
    for ref in pieces:
        for tile in range(ref.shape[1] // LANES):
            here = slice(first + tile * LANES, first + (tile + 1) * LANES)
            value = ref[:, tile * LANES : (tile + 1) * LANES] * scale * gain_ref[:, here]
            out_ref[:, here] = value.astype(bf16)
        first += ref.shape[1]


def moved(block, axis, steps):
    count = lax.axis_size(axis)
    return lax.ppermute(block, axis, [(i, (i + steps) % count) for i in range(count)])


def after(value, *others):
    return lax.optimization_barrier((value, *others))[0]


def packed_state(state, bound):
    power = jnp.ceil(jnp.log2(bound))
    rows = jnp.broadcast_to(power, (8, state.shape[1]))
    return jnp.concatenate([state * jnp.exp2(-power), rows], 0).astype(jnp.float16)


def unpacked(packet):
    wide = packet.astype(f32)
    scale = jnp.exp2(wide[-1:])
    return wide[:-8] * scale, scale


def cut(tiles, shares):
    cuts = sorted({0, *(round(tiles * share) for share in shares), tiles})
    return list(zip(cuts, cuts[1:]))


def body(xs, gate_in, bc_in, dt_in, placement, lengths, conv_x, conv_bc, a_log, dt_bias, d_skip, norm_gain):
    shards = lax.axis_size("seq")
    groups = lax.axis_size("head")
    rows, inner = xs.shape
    width = conv_x.shape[0]
    heads = a_log.shape[0]
    head_dim = inner // heads
    state = bc_in.shape[1] // 2
    per = rows // shards
    group = per + RIM
    tiles = inner // TILE
    chunks = rows // CHUNK
    parts = cut(tiles, SHARES)
    gate_parts = cut(tiles, GATE_SHARES)
    triple = jnp.stack([dt_bias, a_log, d_skip])
    lines = jnp.pad(jnp.concatenate([triple] * GROUPS, 1), ((0, 5), (0, LANES - GROUPS * heads)))

    place = placement.reshape(1, rows)
    thin = dt_in.T
    full = rows + shards * RIM
    quarter = 2 * state // groups
    first, last = parts[0]
    sent = call(
        functools.partial(send_order, shards, width, quarter),
        [shape(full, rows)] + [shape(group, LANES)] * shards + [shape(group, (last - first) * TILE)] * shards,
        (place, bc_in, thin, xs),
        [whole(place), whole(bc_in), whole(thin), columns(rows)],
        [whole(shape(full, rows))] + [whole(shape(group, LANES))] * shards + [columns(group)] * shards,
        grid=(last - first,),
        micros=7,
        limit=56,
    )
    picks, small, x_send = sent[0], sent[1 : 1 + shards], [sent[1 + shards :]]
    small = [small[0]] + [moved(small[k], "seq", k) for k in range(1, shards)]
    arrived = [[x_send[0][0]] + [moved(x_send[0][k], "seq", k) for k in range(1, shards)]]

    small = [jnp.concatenate(small, 0)]
    mask = groups // 2
    while mask:
        held = jnp.concatenate(small, 0) if len(small) > 1 else small[0]
        small.append(lax.ppermute(held, "head", [(i, i ^ mask) for i in range(groups)]))
        mask //= 2
    for first, last in parts[1:]:
        x_send.append(
            call(
                functools.partial(gather_rows, shards, True),
                [shape(group, (last - first) * TILE)] * shards,
                (picks, xs),
                [whole(picks), columns(rows, start=first)],
                [columns(group)] * shards,
                grid=(last - first,),
                micros=2 * (last - first),
            )
        )
    def within(first, last):
        return pl.BlockSpec((per, TILE), lambda j: (0, jnp.clip(j - first, 0, last - first - 1)))

    gate_send = call(
        functools.partial(gather_parts, shards, gate_parts),
        [shape(per, (last - first) * TILE) for first, last in gate_parts for _ in range(shards)],
        (picks, gate_in),
        [whole(shape(rows, rows)), columns(rows)],
        [within(first, last) for first, last in gate_parts for _ in range(shards)],
        grid=(tiles,),
        micros=2 * tiles,
    )
    gate_send = [gate_send[number * shards : (number + 1) * shards] for number in range(len(gate_parts))]

    kept = [
        shape(rows, rows),
        shape(RIM, shards * RIM),
        shape(rows, LANES, dtype=jnp.int32),
        shape(rows, ROWS),
        shape(rows, ROWS),
        shape(rows, state),
        shape(rows, state),
        shape(state, rows),
        shape(rows, LANES),
        shape(rows, LANES),
        shape(rows, LANES),
        shape(LANES, inner),
        shape(chunks, inner, dtype=f32),
        shape(8, inner, dtype=f32),
    ]
    (
        pick, rims, gap, score_high, score_low, query, kept_query,
        keys, inside, outside, carried, expand, factor, rest,
    ) = call(
        functools.partial(prepare, shards, groups, width, heads, head_dim),
        kept,
        (lengths, small[0], conv_bc, lines, *small[1:]),
        [smem()] + [whole(s) for s in (small[0], conv_bc, lines, *small[1:])],
        [whole(s) for s in kept],
        scratch=[
            pltpu.VMEM((rows + HALO, 2 * state), f32),
            pltpu.VMEM((rows, LANES), f32),
            pltpu.VMEM((rows, LANES), f32),
        ],
        micros=8,
    )

    distances = sorted(range(1, shards), key=lambda k: (abs(2 * k - shards), k))

    def stream(send, before, *others):
        return [send[0]] + [
            moved(after(send[k], before[k], *others), "seq", k) for k in range(1, shards)
        ]

    if len(parts) > 1:
        arrived.append(stream(x_send[1], arrived[0], gate_send[0][0], x_send[-1][0]))

    scans, ends, states, gates = [], [], [], []
    for number, part in enumerate(parts):
        blocks = arrived[number]
        first, last = part
        size = (last - first) * TILE
        if ends:
            blocks = [after(blocks[0], ends[-1])] + blocks[1:]
        scanned, local_state, largest = call(
            functools.partial(scan_columns, shards, width),
            [shape(rows, size, dtype=f32), shape(state, size, dtype=f32), shape(8, size, dtype=f32)],
            (
                lengths, pick, rims, gap, score_high, score_low, kept_query, keys, inside, outside,
                expand, factor, rest, conv_x, *blocks,
            ),
            [smem()]
            + [whole(a) for a in (pick, rims, gap, score_high, score_low, kept_query, keys, inside, outside)]
            + [columns(n, start=first) for n in (LANES, chunks, 8, width)]
            + [columns(group)] * shards,
            [columns(rows), columns(state), columns(8)],
            grid=(last - first,),
            scratch=[pltpu.VMEM((rows, TILE), bf16), pltpu.VMEM((rows + HALO, TILE), f32)],
            micros=5 * (last - first),
        )
        scans.append(scanned)
        ends.append(local_state)
        if number + 2 < len(parts):
            arrived.append(stream(x_send[number + 2], arrived[number + 1], local_state))
        if not gates and number + 2 >= len(parts):
            started = [(arrived[-1][k], local_state) for k in distances[:WINDOW]]
            for send in gate_send:
                gates.append([send[0]] + [None] * (shards - 1))
                for k in distances:
                    block = moved(after(send[k], *started[-WINDOW]), "seq", k)
                    gates[-1][k] = block
                    started.append((block,))
        following = (arrived + gates)[number + 1][distances[0]]
        local_state = after(local_state, following)
        passing = rest[0:1, first * TILE : last * TILE]
        packet = None
        for step in range(1, shards):
            leaving, bound = local_state, largest[0:1]
            if packet is not None:
                incoming, reach = unpacked(packet)
                leaving, bound = leaving + passing * incoming, bound + passing * reach
            received = lax.ppermute(packed_state(leaving, bound), "seq", [(step - 1, step)])
            packet = received if packet is None else packet + received
        states.append(unpacked(packet)[0])

    outs, totals = [], [jnp.zeros((1, rows), f32)]
    for tile in range(tiles):
        part = sum(tile >= last for _, last in parts)
        gate_part = sum(tile >= last for _, last in gate_parts)
        blocks = gates[gate_part]
        if gate_part + 1 < len(gates):
            blocks = [after(blocks[0], gates[gate_part + 1][distances[0]])] + blocks[1:]
        gated, total = call(
            functools.partial(gate_columns, shards),
            [shape(rows, TILE, dtype=f32), shape(1, rows, dtype=f32)],
            (totals[-1], pick, query, carried, expand, scans[part], states[part], *blocks),
            [whole(totals[-1]), whole(pick), whole(query), whole(carried), columns(LANES, start=tile)]
            + [columns(n, start=tile - parts[part][0]) for n in (rows, state)]
            + [columns(per, start=tile - gate_parts[gate_part][0])] * shards,
            [columns(rows), whole(shape(1, rows))],
            scratch=[pltpu.VMEM((rows, TILE), bf16), pltpu.VMEM((rows, LANES), f32)],
            micros=3,
        )
        outs.append(gated)
        totals.append(total)
    total = [totals[-1]] + [moved(totals[-1], "head", k) for k in range(1, groups)]
    gain = norm_gain.reshape(1, inner)
    return call(
        functools.partial(normalize, inner * groups, groups),
        shape(rows, inner),
        (*total, gain, *outs),
        [pl.BlockSpec((1, ROWS), lambda i: (0, i))] * groups + [whole(gain)]
        + [pl.BlockSpec((ROWS, out.shape[1]), lambda i: (i, 0)) for out in outs],
        pl.BlockSpec((ROWS, inner), lambda i: (i, 0)),
        grid=(rows // ROWS,),
        micros=5,
    )


def solution(mesh):
    in_specs = (
        P(("parts", "seq"), "head"),
        P(("parts", "seq"), "head"),
        P(("parts", "seq"), None),
        P(("parts", "seq"), "head"),
        P(("parts", "seq")),
        P("parts"),
        P(None, "head"),
        P(),
        P("head"),
        P("head"),
        P("head"),
        P("head"),
    )
    out_specs = P(("parts", "seq"), "head")
    return jax.shard_map(body, mesh=mesh, in_specs=in_specs, out_specs=out_specs, check_vma=False)
```

```python
import functools

import jax
import jax.numpy as jnp
from jax import lax
from jax.experimental import pallas as pl
from jax.experimental.pallas import tpu as pltpu
from jax.sharding import PartitionSpec as P

CHUNK = 64
ROWS = 256
TILE = 256
LANES = 128
RIM = 16
SHARES = (0.4,)
GATE_SHARES = (0.6,)
WINDOW = 2
TINY = 2.0**-100
HALO = 8
GROUPS = 3
FAR = 1 << 28
FLOPS_US = 1_150_000_000
bf16 = jnp.bfloat16
f32 = jnp.float32


def dot(a, b):
    return jnp.dot(a, b, preferred_element_type=f32)


def dot_nt(a, b):
    return lax.dot_general(a, b, (((1,), (1,)), ((), ())), preferred_element_type=f32)


def iota(shape, dim):
    return lax.broadcasted_iota(jnp.int32, shape, dim)


def ones_where(mask):
    return jnp.where(mask, 1.0, 0.0).astype(bf16)


def high_low(value):
    high = value.astype(bf16)
    return high, (value - high.astype(f32)).astype(bf16)


def split_lanes(value, heads):
    lane = iota(value.shape, 1)
    high = value.astype(bf16).astype(f32)
    rest = value - high
    middle = rest.astype(bf16).astype(f32)
    lowest = rest - middle
    pieces = jnp.where(lane < heads, high, jnp.where(lane < 2 * heads, middle, lowest))
    return jnp.where(lane < GROUPS * heads, pieces, 0.0).astype(bf16)


def silu(value):
    return value * jax.nn.sigmoid(value)


def call(kernel, outs, args, in_specs, out_specs, grid=(1,), scratch=(), micros=1, limit=24):
    return pl.pallas_call(
        kernel,
        grid=grid,
        in_specs=in_specs,
        out_specs=out_specs,
        out_shape=outs,
        scratch_shapes=list(scratch),
        compiler_params=pltpu.CompilerParams(vmem_limit_bytes=limit * 1024 * 1024),
        cost_estimate=pl.CostEstimate(flops=int(micros * FLOPS_US), bytes_accessed=0, transcendentals=0),
    )(*args)


def whole(array):
    rank = len(array.shape)
    return pl.BlockSpec(array.shape, lambda *_: (0,) * rank)


def columns(rows, width=TILE, start=0):
    return pl.BlockSpec((rows, width), lambda j: (0, j + start))


def smem():
    return pl.BlockSpec(memory_space=pltpu.SMEM)


def shape(*dims, dtype=bf16):
    return jax.ShapeDtypeStruct(dims, dtype)


def send_order(shards, width, quarter, place_ref, bc_ref, dt_ref, x_ref, pick_ref, *refs):
    small_refs, x_refs = refs[:shards], refs[shards:]
    rows = place_ref.shape[1]
    per = rows // shards
    heads = dt_ref.shape[0]
    both = bc_ref.shape[1]

    @pl.when(pl.program_id(0) == 0)
    def _():
        me = lax.axis_index("seq")
        place = place_ref[...]
        padded = max(8, shards)
        owner = iota((padded, rows), 0)
        first = owner * rows
        mine = (place >= first) & (place < first + rows)
        chosen = ones_where(mine)
        earlier = ones_where(iota((LANES, LANES), 0) < iota((LANES, LANES), 1))
        before, seen = [], jnp.zeros((padded, 1), f32)
        for piece in range(rows // LANES):
            part = chosen[:, piece * LANES : (piece + 1) * LANES]
            before.append(dot(part, earlier) + seen)
            seen = seen + jnp.sum(part.astype(f32), axis=1, keepdims=True)
        before = jnp.concatenate(before, 1)
        relative = jnp.where(owner >= me, owner - me, owner - me + shards)
        target = before + (relative * per).astype(f32)
        target = jnp.sum(jnp.where(mine, target, 0.0), axis=0, keepdims=True).astype(jnp.int32)
        local = jnp.sum(jnp.where(mine, (place - first + 1).astype(f32), 0.0), axis=0, keepdims=True)
        high = jnp.floor(local * (1.0 / 64.0))
        low = local - 64.0 * high
        line = iota((LANES - quarter - heads, rows), 0)
        digits = jnp.where(line == 0, high, jnp.where(line == 1, low, 0.0)).astype(bf16)
        thin = jnp.concatenate([jnp.zeros((quarter, rows), bf16), dt_ref[...], digits], 0)
        own = lax.axis_index("head") * quarter
        lane = iota((both, LANES), 1)
        taken = ones_where((iota((both, LANES), 0) == lane + own) & (lane < quarter))
        thick = dot(bc_ref[...], taken).astype(bf16)
        for k in range(shards):
            pick = ones_where(iota((per, rows), 0) + k * per == target)
            pick_ref[k * per : (k + 1) * per] = pick
            dest = jnp.where(me + k >= shards, me + k - shards, me + k)
            row = iota((RIM, rows), 0)
            rim = ones_where((row < width - 1) & (place == row + (dest * rows - (width - 1))))
            pick_ref[rows + k * RIM : rows + (k + 1) * RIM] = rim
            small_refs[k][:per] = (dot(pick, thick) + dot_nt(pick, thin)).astype(bf16)
            small_refs[k][per:] = (dot(rim, thick) + dot_nt(rim, thin)).astype(bf16)

    gather_rows(shards, True, pick_ref, x_ref, *x_refs)


def gather_rows(shards, with_rim, pick_ref, x_ref, *out_refs):
    rows = x_ref.shape[0]
    per = rows // shards
    values = x_ref[...]
    for k in range(shards):
        out_refs[k][:per] = dot(pick_ref[k * per : (k + 1) * per], values).astype(bf16)
    if with_rim:
        rims = dot(pick_ref[rows:], values).astype(bf16)
        for k in range(shards):
            out_refs[k][per:] = rims[k * RIM : (k + 1) * RIM]


def gather_parts(shards, parts, pick_ref, x_ref, *out_refs):
    rows = x_ref.shape[0]
    per = rows // shards
    values = x_ref[...]
    for number, (first, last) in enumerate(parts):

        @pl.when((pl.program_id(0) >= first) & (pl.program_id(0) < last))
        def _():
            for k in range(shards):
                taken = dot(pick_ref[k * per : (k + 1) * per], values)
                out_refs[number * shards + k][...] = taken.astype(bf16)


def distance(position, lengths, limit):
    gap, start = limit, 0
    for j in range(lengths.shape[0]):
        gap = jnp.where(position >= start, jnp.minimum(gap, position - start), gap)
        start = start + lengths[j]
    return gap


def convolve(block_of, taps, gap, width):
    total = taps[0:1] * block_of(0)
    for lag in range(1, width):
        total = total + jnp.where(gap >= lag, taps[lag : lag + 1] * block_of(lag), 0.0)
    return silu(total).astype(bf16)


def prepare(
    shards, groups, width, heads, head_dim, lengths, first_ref, taps_ref, lines_ref, *refs
):
    (
        pick_ref, rims_ref, gap_ref, score_high_ref, score_low_ref, query_ref, kept_query_ref,
        keys_ref, inside_ref, outside_ref, carried_ref, expand_ref, factor_ref, rest_ref,
        packed, log_sums, steps,
    ) = refs[-17:]
    others = refs[:-17]
    rows = pick_ref.shape[0]
    per = rows // shards
    group = per + RIM
    state = query_ref.shape[1]
    base = lax.axis_index("seq") * rows
    sources = [first_ref]
    flips = [0]
    for ref in others:
        flips = flips + [flip ^ (groups // (2 * len(flips))) for flip in flips]
        sources = sources + [ref.at[n * shards * group : (n + 1) * shards * group] for n in range(len(sources))]
    quarter = 2 * state // len(sources)

    def main(ref):
        return jnp.concatenate([ref[k * group : k * group + per] for k in range(shards)], 0)

    def rim(ref):
        return jnp.concatenate([ref[k * group + per : (k + 1) * group] for k in range(shards)], 0)

    own_main = main(first_ref)
    lane = iota((8, LANES), 1)
    high_lane = quarter + heads
    weights = jnp.where(lane == high_lane, 64.0, jnp.where(lane == high_lane + 1, 1.0, 0.0)).astype(bf16)
    slots = dot_nt(weights, own_main)[0:1].astype(jnp.int32) - 1
    rim_slots = dot_nt(weights, rim(first_ref))[0:1].astype(jnp.int32) - 1 - rows + HALO
    rim_pick = ones_where(iota((RIM, shards * RIM), 0) == rim_slots)
    rims_ref[...] = rim_pick
    me = lax.axis_index("head")
    bc_main, bc_rim = 0.0, 0.0
    for flip, ref in zip(flips, sources):
        lane = iota((LANES, 2 * state), 0)
        spread = ones_where((lane < quarter) & (lane + (me ^ flip) * quarter == iota((LANES, 2 * state), 1)))
        bc_main = bc_main + dot(main(ref), spread)
        bc_rim = bc_rim + dot(rim(ref), spread)
    bc_main = bc_main.astype(bf16)
    packed[0:HALO] = dot(rim_pick, bc_rim.astype(bf16))[0:HALO]
    lane_of = iota((LANES, LANES), 0) - quarter
    wide = iota((LANES, LANES), 1)
    copy_dt = ones_where(
        (lane_of >= 0) & (lane_of < heads)
        & ((lane_of == wide) | (lane_of + heads == wide) | (lane_of + 2 * heads == wide))
    )
    decay_rate = -jnp.exp(lines_ref[1:2])
    row_in = iota((ROWS, ROWS), 0)
    col_in = iota((ROWS, ROWS), 1)
    same_chunk = (row_in // CHUNK) == (col_in // CHUNK)
    lower = same_chunk & (col_in <= row_in)
    sums = ones_where(lower)
    expand = iota((LANES, heads * head_dim), 0)
    head_of = jnp.where(expand >= 2 * heads, expand - 2 * heads, jnp.where(expand >= heads, expand - heads, expand))
    channel = iota((LANES, heads * head_dim), 1)
    expand = ones_where(
        (expand < GROUPS * heads) & (channel >= head_of * head_dim) & (channel < (head_of + 1) * head_dim)
    )
    expand_ref[...] = expand
    for b in range(rows // ROWS):
        here = slice(b * ROWS, (b + 1) * ROWS)
        pick = ones_where(iota((ROWS, rows), 0) + b * ROWS == slots)
        pick_ref[here] = pick
        packed[HALO + b * ROWS : HALO + (b + 1) * ROWS] = dot(pick, bc_main)
        raw = dot(pick, own_main).astype(bf16)
        step = jax.nn.softplus(dot(raw, copy_dt) + lines_ref[0:1])
        log_decay = decay_rate * step
        high = log_decay.astype(bf16)
        rest = log_decay - high.astype(f32)
        middle = rest.astype(bf16)
        lowest = (rest - middle.astype(f32)).astype(bf16)
        log_sums[here] = dot(sums, high) + dot(sums, middle) + dot(sums, lowest)
        steps[here] = step
    total = jnp.zeros((1, LANES), f32)
    chunks = rows // CHUNK
    factors = []
    pending = None
    for c in range(chunks):
        here = slice(c * CHUNK, (c + 1) * CHUNK)
        logs = log_sums[here]
        centre = logs[CHUNK // 2 - 1 : CHUNK // 2]
        last = logs[CHUNK - 1 : CHUNK]
        outside_ref[here] = split_lanes(jnp.exp(logs - centre), heads)
        inside_ref[here] = split_lanes(jnp.exp(centre - logs) * steps[here], heads)
        offset = iota((CHUNK, LANES), 0) + c * CHUNK
        gap = distance(offset + base, lengths, FAR)
        gap_ref[here] = gap
        carried_ref[here] = split_lanes(jnp.where(gap > offset, jnp.exp(logs + total), 0.0), heads)
        if pending is not None:
            factors.append(jnp.exp(pending + centre))
        pending = last - centre
        total = total + last
    factors.append(jnp.exp(pending))
    end_gap = distance(base + rows - 1, lengths, FAR)
    decay = jnp.where(end_gap >= rows, jnp.exp(total), 0.0)
    for c in range(chunks):
        log_sums[c : c + 1] = factors[c]
    factor_ref[...] = dot(split_lanes(log_sums[0:chunks], heads), expand)
    log_sums[0:1] = decay
    log_sums[1:2] = lines_ref[2:3]
    rest_ref[...] = dot(split_lanes(log_sums[0:8], heads), expand)
    for b in range(rows // ROWS):
        here = slice(b * ROWS, (b + 1) * ROWS)
        gap = gap_ref[here]
        wide_gap = jnp.concatenate([gap] * (2 * state // LANES), 1)

        def shifted(lag):
            return packed[HALO + b * ROWS - lag : HALO + (b + 1) * ROWS - lag]

        both = convolve(shifted, taps_ref[...], wide_gap, width)
        keys, queries = both[:, :state], both[:, state:]
        query_ref[here] = queries
        offset = iota((ROWS, state), 0)
        in_chunk = offset % CHUNK
        zero = jnp.zeros_like(queries)
        kept_query_ref[here] = jnp.where(gap > in_chunk, queries.astype(f32), 0.0).astype(bf16)
        ends = jnp.zeros((ROWS, state), jnp.int32)
        for c in range(ROWS // CHUNK):
            end = base + b * ROWS + (c + 1) * CHUNK - 1
            ends = jnp.where(offset // CHUNK == c, distance(end, lengths, FAR), ends)
        last_keys = jnp.where(CHUNK - 1 - in_chunk <= ends, keys.astype(f32), 0.0)
        keys_ref[:, here] = last_keys.T.astype(bf16)
        scores = dot_nt(queries, keys)
        gap_square = jnp.concatenate([gap] * (ROWS // LANES), 1)
        scores = jnp.where(lower & (row_in - col_in <= gap_square), scores, 0.0)
        high, low = high_low(scores)
        score_high_ref[here] = high
        score_low_ref[here] = low


def scan_columns(
    shards, width,
    lengths, pick_ref, rims_ref, gap_ref, score_high_ref, score_low_ref, kept_query_ref, keys_ref,
    inside_ref, outside_ref, expand_ref, factor_ref, rest_ref, taps_ref, *refs,
):
    blocks = refs[:shards]
    out_ref, state_ref, size_ref, arrived, packed = refs[shards:]
    rows = pick_ref.shape[0]
    per = rows // shards
    base = lax.axis_index("seq") * rows
    for k in range(shards):
        arrived[k * per : (k + 1) * per] = blocks[k][:per]
    rim = jnp.concatenate([blocks[k][per:] for k in range(shards)], 0)
    packed[0:HALO] = dot(rims_ref[...], rim)[0:HALO]
    expand = expand_ref[...]
    state_ref[...] = jnp.zeros_like(state_ref)
    for b in range(rows // ROWS):
        here = slice(b * ROWS, (b + 1) * ROWS)
        packed[HALO + b * ROWS : HALO + (b + 1) * ROWS] = dot(pick_ref[here], arrived[...])
        gap = gap_ref[here]

        def shifted(lag):
            return packed[HALO + b * ROWS - lag : HALO + (b + 1) * ROWS - lag]

        conv = convolve(shifted, taps_ref[...], jnp.concatenate([gap] * (TILE // LANES), 1), width).astype(f32)
        scaled = conv * dot(inside_ref[here], expand)
        high, low = high_low(scaled)
        score_high, score_low = score_high_ref[here], score_low_ref[here]
        total = dot(score_high, high) + dot(score_low, high) + dot(score_high, low)
        outside = dot(outside_ref[here], expand)
        carry = state_ref[...]
        parts = []
        for c in range(ROWS // CHUNK):
            inner = slice(c * CHUNK, (c + 1) * CHUNK)
            place = slice(b * ROWS + c * CHUNK, b * ROWS + (c + 1) * CHUNK)
            carry_high, carry_low = high_low(carry)
            kept = kept_query_ref[place]
            parts.append(dot(kept, carry_high) + dot(kept, carry_low))
            keys = keys_ref[:, place]
            added = dot(keys, high[inner]) + dot(keys, low[inner])
            end = base + b * ROWS + (c + 1) * CHUNK - 1
            keep = jnp.where(distance(end, lengths, FAR) >= CHUNK, 1.0, 0.0)
            number = b * (ROWS // CHUNK) + c
            carry = (carry * keep + added) * factor_ref[number : number + 1]
        state_ref[...] = carry
        out_ref[here] = outside * (total + jnp.concatenate(parts, 0)) + rest_ref[1:2] * conv
    largest = jnp.max(jnp.abs(state_ref[...]), axis=0, keepdims=True)
    size_ref[...] = jnp.broadcast_to(jnp.maximum(largest, TINY), size_ref.shape)


def gate_columns(shards, sum_ref, pick_ref, query_ref, carried_ref, expand_ref, scan_ref, state_ref, *refs):
    blocks = refs[:shards]
    out_ref, total_ref, arrived, square_ref = refs[shards:]
    rows = pick_ref.shape[0]
    per = rows // shards
    for k in range(shards):
        arrived[k * per : (k + 1) * per] = blocks[k][...]

    @pl.when(pl.program_id(0) == 0)
    def _():
        square_ref[...] = jnp.zeros_like(square_ref)

    carry_high, carry_low = high_low(state_ref[...])
    for b in range(rows // ROWS):
        here = slice(b * ROWS, (b + 1) * ROWS)
        gate = dot(pick_ref[here], arrived[...])
        queries = query_ref[here]
        earlier = dot(queries, carry_high) + dot(queries, carry_low)
        outputs = scan_ref[here] + dot(carried_ref[here], expand_ref[...]) * earlier
        gated = outputs * silu(gate)
        out_ref[here] = gated
        squares = gated * gated
        part = squares[:, :LANES]
        for piece in range(1, TILE // LANES):
            part = part + squares[:, piece * LANES : (piece + 1) * LANES]
        square_ref[here] = square_ref[here] + part

    @pl.when(pl.program_id(0) == pl.num_programs(0) - 1)
    def _():
        for b in range(rows // ROWS):
            here = slice(b * ROWS, (b + 1) * ROWS)
            total_ref[:, here] = sum_ref[:, here] + jnp.sum(square_ref[here].T, axis=0, keepdims=True)


def normalize(count, groups, *refs):
    pieces, out_ref = refs[groups + 1 : -1], refs[-1]
    gain_ref = refs[groups]
    scale = refs[0][...]
    for ref in refs[1:groups]:
        scale = scale + ref[...]
    scale = lax.rsqrt(scale / count + 1e-05)
    scale = jnp.broadcast_to(scale, (LANES, scale.shape[1])).T
    first = 0
    for ref in pieces:
        for tile in range(ref.shape[1] // LANES):
            here = slice(first + tile * LANES, first + (tile + 1) * LANES)
            value = ref[:, tile * LANES : (tile + 1) * LANES] * scale * gain_ref[:, here]
            out_ref[:, here] = value.astype(bf16)
        first += ref.shape[1]


def moved(block, axis, steps):
    count = lax.axis_size(axis)
    return lax.ppermute(block, axis, [(i, (i + steps) % count) for i in range(count)])


def after(value, *others):
    return lax.optimization_barrier((value, *others))[0]


def packed_state(state, bound):
    power = jnp.ceil(jnp.log2(bound))
    rows = jnp.broadcast_to(power, (8, state.shape[1]))
    return jnp.concatenate([state * jnp.exp2(-power), rows], 0).astype(jnp.float16)


def unpacked(packet):
    wide = packet.astype(f32)
    scale = jnp.exp2(wide[-1:])
    return wide[:-8] * scale, scale


def cut(tiles, shares):
    cuts = sorted({0, *(round(tiles * share) for share in shares), tiles})
    return list(zip(cuts, cuts[1:]))


def body(xs, gate_in, bc_in, dt_in, placement, lengths, conv_x, conv_bc, a_log, dt_bias, d_skip, norm_gain):
    shards = lax.axis_size("seq")
    groups = lax.axis_size("head")
    rows, inner = xs.shape
    width = conv_x.shape[0]
    heads = a_log.shape[0]
    head_dim = inner // heads
    state = bc_in.shape[1] // 2
    per = rows // shards
    group = per + RIM
    tiles = inner // TILE
    chunks = rows // CHUNK
    parts = cut(tiles, SHARES)
    gate_parts = cut(tiles, GATE_SHARES)
    triple = jnp.stack([dt_bias, a_log, d_skip])
    lines = jnp.pad(jnp.concatenate([triple] * GROUPS, 1), ((0, 5), (0, LANES - GROUPS * heads)))

    place = placement.reshape(1, rows)
    thin = dt_in.T
    full = rows + shards * RIM
    quarter = 2 * state // groups
    first, last = parts[0]
    sent = call(
        functools.partial(send_order, shards, width, quarter),
        [shape(full, rows)] + [shape(group, LANES)] * shards + [shape(group, (last - first) * TILE)] * shards,
        (place, bc_in, thin, xs),
        [whole(place), whole(bc_in), whole(thin), columns(rows)],
        [whole(shape(full, rows))] + [whole(shape(group, LANES))] * shards + [columns(group)] * shards,
        grid=(last - first,),
        micros=7,
        limit=56,
    )
    picks, small, x_send = sent[0], sent[1 : 1 + shards], [sent[1 + shards :]]
    small = [small[0]] + [moved(small[k], "seq", k) for k in range(1, shards)]
    distances = list(range(shards - 1, 0, -1))
    started = []

    def queued(send, *others):
        received = [send[0]] + [None] * (shards - 1)
        for k in distances:
            waits = [started[-WINDOW]] if len(started) >= shards - 1 else []
            received[k] = moved(after(send[k], *waits, *others), "seq", k)
            started.append(received[k])
        return received

    arrived = [queued(x_send[0])]

    small = [jnp.concatenate(small, 0)]
    mask = groups // 2
    while mask:
        held = jnp.concatenate(small, 0) if len(small) > 1 else small[0]
        small.append(lax.ppermute(held, "head", [(i, i ^ mask) for i in range(groups)]))
        mask //= 2
    for first, last in parts[1:]:
        x_send.append(
            call(
                functools.partial(gather_rows, shards, True),
                [shape(group, (last - first) * TILE)] * shards,
                (picks, xs),
                [whole(picks), columns(rows, start=first)],
                [columns(group)] * shards,
                grid=(last - first,),
                micros=2 * (last - first),
            )
        )
    def within(first, last):
        return pl.BlockSpec((per, TILE), lambda j: (0, jnp.clip(j - first, 0, last - first - 1)))

    gate_send = call(
        functools.partial(gather_parts, shards, gate_parts),
        [shape(per, (last - first) * TILE) for first, last in gate_parts for _ in range(shards)],
        (picks, gate_in),
        [whole(shape(rows, rows)), columns(rows)],
        [within(first, last) for first, last in gate_parts for _ in range(shards)],
        grid=(tiles,),
        micros=2 * tiles,
    )
    gate_send = [gate_send[number * shards : (number + 1) * shards] for number in range(len(gate_parts))]

    kept = [
        shape(rows, rows),
        shape(RIM, shards * RIM),
        shape(rows, LANES, dtype=jnp.int32),
        shape(rows, ROWS),
        shape(rows, ROWS),
        shape(rows, state),
        shape(rows, state),
        shape(state, rows),
        shape(rows, LANES),
        shape(rows, LANES),
        shape(rows, LANES),
        shape(LANES, inner),
        shape(chunks, inner, dtype=f32),
        shape(8, inner, dtype=f32),
    ]
    (
        pick, rims, gap, score_high, score_low, query, kept_query,
        keys, inside, outside, carried, expand, factor, rest,
    ) = call(
        functools.partial(prepare, shards, groups, width, heads, head_dim),
        kept,
        (lengths, small[0], conv_bc, lines, *small[1:]),
        [smem()] + [whole(s) for s in (small[0], conv_bc, lines, *small[1:])],
        [whole(s) for s in kept],
        scratch=[
            pltpu.VMEM((rows + HALO, 2 * state), f32),
            pltpu.VMEM((rows, LANES), f32),
            pltpu.VMEM((rows, LANES), f32),
        ],
        micros=8,
    )

    if len(parts) > 1:
        arrived.append(queued(x_send[1], gate_send[0][0], x_send[-1][0]))

    scans, ends, states, gates = [], [], [], []
    for number, part in enumerate(parts):
        blocks = arrived[number]
        first, last = part
        size = (last - first) * TILE
        if ends:
            blocks = [after(blocks[0], ends[-1])] + blocks[1:]
        scanned, local_state, largest = call(
            functools.partial(scan_columns, shards, width),
            [shape(rows, size, dtype=f32), shape(state, size, dtype=f32), shape(8, size, dtype=f32)],
            (
                lengths, pick, rims, gap, score_high, score_low, kept_query, keys, inside, outside,
                expand, factor, rest, conv_x, *blocks,
            ),
            [smem()]
            + [whole(a) for a in (pick, rims, gap, score_high, score_low, kept_query, keys, inside, outside)]
            + [columns(n, start=first) for n in (LANES, chunks, 8, width)]
            + [columns(group)] * shards,
            [columns(rows), columns(state), columns(8)],
            grid=(last - first,),
            scratch=[pltpu.VMEM((rows, TILE), bf16), pltpu.VMEM((rows + HALO, TILE), f32)],
            micros=5 * (last - first),
        )
        scans.append(scanned)
        ends.append(local_state)
        if number + 2 < len(parts):
            arrived.append(queued(x_send[number + 2], local_state))
        if not gates and number + 2 >= len(parts):
            gates = [queued(send, local_state) for send in gate_send]
        following = (arrived + gates)[number + 1][distances[0]]
        local_state = after(local_state, following)
        passing = rest[0:1, first * TILE : last * TILE]
        packet = None
        for step in range(1, shards):
            leaving, bound = local_state, largest[0:1]
            if packet is not None:
                incoming, reach = unpacked(packet)
                leaving, bound = leaving + passing * incoming, bound + passing * reach
            received = lax.ppermute(packed_state(leaving, bound), "seq", [(step - 1, step)])
            packet = received if packet is None else packet + received
        states.append(unpacked(packet)[0])

    outs, totals = [], [jnp.zeros((1, rows), f32)]
    for tile in range(tiles):
        part = sum(tile >= last for _, last in parts)
        gate_part = sum(tile >= last for _, last in gate_parts)
        blocks = gates[gate_part]
        if gate_part + 1 < len(gates):
            blocks = [after(blocks[0], gates[gate_part + 1][distances[0]])] + blocks[1:]
        gated, total = call(
            functools.partial(gate_columns, shards),
            [shape(rows, TILE, dtype=f32), shape(1, rows, dtype=f32)],
            (totals[-1], pick, query, carried, expand, scans[part], states[part], *blocks),
            [whole(totals[-1]), whole(pick), whole(query), whole(carried), columns(LANES, start=tile)]
            + [columns(n, start=tile - parts[part][0]) for n in (rows, state)]
            + [columns(per, start=tile - gate_parts[gate_part][0])] * shards,
            [columns(rows), whole(shape(1, rows))],
            scratch=[pltpu.VMEM((rows, TILE), bf16), pltpu.VMEM((rows, LANES), f32)],
            micros=3,
        )
        outs.append(gated)
        totals.append(total)
    total = [totals[-1]] + [moved(totals[-1], "head", k) for k in range(1, groups)]
    gain = norm_gain.reshape(1, inner)
    return call(
        functools.partial(normalize, inner * groups, groups),
        shape(rows, inner),
        (*total, gain, *outs),
        [pl.BlockSpec((1, ROWS), lambda i: (0, i))] * groups + [whole(gain)]
        + [pl.BlockSpec((ROWS, out.shape[1]), lambda i: (i, 0)) for out in outs],
        pl.BlockSpec((ROWS, inner), lambda i: (i, 0)),
        grid=(rows // ROWS,),
        micros=5,
    )


def solution(mesh):
    in_specs = (
        P(("parts", "seq"), "head"),
        P(("parts", "seq"), "head"),
        P(("parts", "seq"), None),
        P(("parts", "seq"), "head"),
        P(("parts", "seq")),
        P("parts"),
        P(None, "head"),
        P(),
        P("head"),
        P("head"),
        P("head"),
        P("head"),
    )
    out_specs = P(("parts", "seq"), "head")
    return jax.shard_map(body, mesh=mesh, in_specs=in_specs, out_specs=out_specs, check_vma=False)
```

```python
import functools

import jax
import jax.numpy as jnp
from jax import lax
from jax.experimental import pallas as pl
from jax.experimental.pallas import tpu as pltpu
from jax.sharding import PartitionSpec as P

CHUNK = 64
ROWS = 256
TILE = 256
LANES = 128
RIM = 16
EDGE = 4
SHARES = (0.4,)
GATE_SHARES = (0.6,)
WINDOW = 2
TINY = 2.0**-100
HALO = 8
GROUPS = 3
FAR = 1 << 28
FLOPS_US = 1_150_000_000
bf16 = jnp.bfloat16
f32 = jnp.float32


def dot(a, b):
    return jnp.dot(a, b, preferred_element_type=f32)


def dot_nt(a, b):
    return lax.dot_general(a, b, (((1,), (1,)), ((), ())), preferred_element_type=f32)


def iota(shape, dim):
    return lax.broadcasted_iota(jnp.int32, shape, dim)


def ones_where(mask):
    return jnp.where(mask, 1.0, 0.0).astype(bf16)


def high_low(value):
    high = value.astype(bf16)
    return high, (value - high.astype(f32)).astype(bf16)


def split_lanes(value, heads):
    lane = iota(value.shape, 1)
    high = value.astype(bf16).astype(f32)
    rest = value - high
    middle = rest.astype(bf16).astype(f32)
    lowest = rest - middle
    pieces = jnp.where(lane < heads, high, jnp.where(lane < 2 * heads, middle, lowest))
    return jnp.where(lane < GROUPS * heads, pieces, 0.0).astype(bf16)


def silu(value):
    return value * jax.nn.sigmoid(value)


def call(kernel, outs, args, in_specs, out_specs, grid=(1,), scratch=(), micros=1, limit=24):
    return pl.pallas_call(
        kernel,
        grid=grid,
        in_specs=in_specs,
        out_specs=out_specs,
        out_shape=outs,
        scratch_shapes=list(scratch),
        compiler_params=pltpu.CompilerParams(vmem_limit_bytes=limit * 1024 * 1024),
        cost_estimate=pl.CostEstimate(flops=int(micros * FLOPS_US), bytes_accessed=0, transcendentals=0),
    )(*args)


def whole(array):
    rank = len(array.shape)
    return pl.BlockSpec(array.shape, lambda *_: (0,) * rank)


def columns(rows, width=TILE, start=0):
    return pl.BlockSpec((rows, width), lambda j: (0, j + start))


def smem():
    return pl.BlockSpec(memory_space=pltpu.SMEM)


def shape(*dims, dtype=bf16):
    return jax.ShapeDtypeStruct(dims, dtype)


def send_order(shards, width, quarter, place_ref, bc_ref, dt_ref, x_ref, pick_ref, *refs):
    small_refs, x_refs = refs[:shards], refs[shards:]
    rows = place_ref.shape[1]
    per = rows // shards
    heads = dt_ref.shape[0]
    both = bc_ref.shape[1]

    @pl.when(pl.program_id(0) == 0)
    def _():
        me = lax.axis_index("seq")
        place = place_ref[...]
        padded = max(8, shards)
        owner = iota((padded, rows), 0)
        first = owner * rows
        mine = (place >= first) & (place < first + rows)
        chosen = ones_where(mine)
        earlier = ones_where(iota((LANES, LANES), 0) < iota((LANES, LANES), 1))
        before, seen = [], jnp.zeros((padded, 1), f32)
        for piece in range(rows // LANES):
            part = chosen[:, piece * LANES : (piece + 1) * LANES]
            before.append(dot(part, earlier) + seen)
            seen = seen + jnp.sum(part.astype(f32), axis=1, keepdims=True)
        before = jnp.concatenate(before, 1)
        relative = jnp.where(owner >= me, owner - me, owner - me + shards)
        target = before + (relative * per).astype(f32)
        target = jnp.sum(jnp.where(mine, target, 0.0), axis=0, keepdims=True).astype(jnp.int32)
        local = jnp.sum(jnp.where(mine, (place - first + 1).astype(f32), 0.0), axis=0, keepdims=True)
        high = jnp.floor(local * (1.0 / 64.0))
        low = local - 64.0 * high
        line = iota((LANES - quarter - heads, rows), 0)
        digits = jnp.where(line == 0, high, jnp.where(line == 1, low, 0.0)).astype(bf16)
        thin = jnp.concatenate([jnp.zeros((quarter, rows), bf16), dt_ref[...], digits], 0)
        own = lax.axis_index("head") * quarter
        lane = iota((both, LANES), 1)
        taken = ones_where((iota((both, LANES), 0) == lane + own) & (lane < quarter))
        thick = dot(bc_ref[...], taken).astype(bf16)
        for k in range(shards):
            pick = ones_where(iota((per, rows), 0) + k * per == target)
            pick_ref[k * per : (k + 1) * per] = pick
            dest = jnp.where(me + k >= shards, me + k - shards, me + k)
            row = iota((RIM, rows), 0)
            rim = ones_where((row < width - 1) & (place == row + (dest * rows - (width - 1))))
            pick_ref[rows + k * RIM : rows + (k + 1) * RIM] = rim
            small_refs[k][:per] = (dot(pick, thick) + dot_nt(pick, thin)).astype(bf16)
            small_refs[k][per:] = (dot(rim, thick) + dot_nt(rim, thin)).astype(bf16)

    gather_rows(shards, pick_ref, x_ref, *x_refs)


def gather_rows(shards, pick_ref, x_ref, *out_refs):
    rows = x_ref.shape[0]
    per = rows // shards
    values = x_ref[...]
    for k in range(shards):
        out_refs[k][...] = dot(pick_ref[k * per : (k + 1) * per], values).astype(bf16)


def gather_rims(pick_ref, x_ref, out_ref):
    out_ref[...] = dot(pick_ref[...], x_ref[...]).astype(bf16)


def gather_parts(shards, parts, pick_ref, x_ref, *out_refs):
    rows = x_ref.shape[0]
    per = rows // shards
    values = x_ref[...]
    for number, (first, last) in enumerate(parts):

        @pl.when((pl.program_id(0) >= first) & (pl.program_id(0) < last))
        def _():
            for k in range(shards):
                taken = dot(pick_ref[k * per : (k + 1) * per], values)
                out_refs[number * shards + k][...] = taken.astype(bf16)


def distance(position, lengths, limit):
    gap, start = limit, 0
    for j in range(lengths.shape[0]):
        gap = jnp.where(position >= start, jnp.minimum(gap, position - start), gap)
        start = start + lengths[j]
    return gap


def convolve(block_of, taps, gap, width):
    total = taps[0:1] * block_of(0)
    for lag in range(1, width):
        total = total + jnp.where(gap >= lag, taps[lag : lag + 1] * block_of(lag), 0.0)
    return silu(total).astype(bf16)


def prepare(
    shards, groups, width, heads, head_dim, lengths, first_ref, taps_ref, lines_ref, *refs
):
    (
        pick_ref, rims_ref, gap_ref, score_high_ref, score_low_ref, query_ref, kept_query_ref,
        keys_ref, inside_ref, outside_ref, carried_ref, expand_ref, factor_ref, rest_ref,
        packed, log_sums, steps,
    ) = refs[-17:]
    others = refs[:-17]
    rows = pick_ref.shape[0]
    per = rows // shards
    group = per + RIM
    state = query_ref.shape[1]
    base = lax.axis_index("seq") * rows
    sources = [first_ref]
    flips = [0]
    for ref in others:
        flips = flips + [flip ^ (groups // (2 * len(flips))) for flip in flips]
        sources = sources + [ref.at[n * shards * group : (n + 1) * shards * group] for n in range(len(sources))]
    quarter = 2 * state // len(sources)

    def main(ref):
        return jnp.concatenate([ref[k * group : k * group + per] for k in range(shards)], 0)

    def rim(ref):
        return jnp.concatenate([ref[k * group + per : (k + 1) * group] for k in range(shards)], 0)

    own_main = main(first_ref)
    lane = iota((8, LANES), 1)
    high_lane = quarter + heads
    weights = jnp.where(lane == high_lane, 64.0, jnp.where(lane == high_lane + 1, 1.0, 0.0)).astype(bf16)
    slots = dot_nt(weights, own_main)[0:1].astype(jnp.int32) - 1
    rim_slots = dot_nt(weights, rim(first_ref))[0:1].astype(jnp.int32) - 1 - rows + HALO
    rim_pick = ones_where(iota((RIM, shards * RIM), 0) == rim_slots)
    source, wanted = iota((shards * RIM, shards * EDGE), 0), iota((shards * RIM, shards * EDGE), 1)
    kept = ones_where((source // RIM == wanted // EDGE) & (source % RIM == wanted % EDGE))
    rims_ref[...] = dot(rim_pick, kept).astype(bf16)
    me = lax.axis_index("head")
    bc_main, bc_rim = 0.0, 0.0
    for flip, ref in zip(flips, sources):
        lane = iota((LANES, 2 * state), 0)
        spread = ones_where((lane < quarter) & (lane + (me ^ flip) * quarter == iota((LANES, 2 * state), 1)))
        bc_main = bc_main + dot(main(ref), spread)
        bc_rim = bc_rim + dot(rim(ref), spread)
    bc_main = bc_main.astype(bf16)
    packed[0:HALO] = dot(rim_pick, bc_rim.astype(bf16))[0:HALO]
    lane_of = iota((LANES, LANES), 0) - quarter
    wide = iota((LANES, LANES), 1)
    copy_dt = ones_where(
        (lane_of >= 0) & (lane_of < heads)
        & ((lane_of == wide) | (lane_of + heads == wide) | (lane_of + 2 * heads == wide))
    )
    decay_rate = -jnp.exp(lines_ref[1:2])
    row_in = iota((ROWS, ROWS), 0)
    col_in = iota((ROWS, ROWS), 1)
    same_chunk = (row_in // CHUNK) == (col_in // CHUNK)
    lower = same_chunk & (col_in <= row_in)
    sums = ones_where(lower)
    expand = iota((LANES, heads * head_dim), 0)
    head_of = jnp.where(expand >= 2 * heads, expand - 2 * heads, jnp.where(expand >= heads, expand - heads, expand))
    channel = iota((LANES, heads * head_dim), 1)
    expand = ones_where(
        (expand < GROUPS * heads) & (channel >= head_of * head_dim) & (channel < (head_of + 1) * head_dim)
    )
    expand_ref[...] = expand
    for b in range(rows // ROWS):
        here = slice(b * ROWS, (b + 1) * ROWS)
        pick = ones_where(iota((ROWS, rows), 0) + b * ROWS == slots)
        pick_ref[here] = pick
        packed[HALO + b * ROWS : HALO + (b + 1) * ROWS] = dot(pick, bc_main)
        raw = dot(pick, own_main).astype(bf16)
        step = jax.nn.softplus(dot(raw, copy_dt) + lines_ref[0:1])
        log_decay = decay_rate * step
        high = log_decay.astype(bf16)
        rest = log_decay - high.astype(f32)
        middle = rest.astype(bf16)
        lowest = (rest - middle.astype(f32)).astype(bf16)
        log_sums[here] = dot(sums, high) + dot(sums, middle) + dot(sums, lowest)
        steps[here] = step
    total = jnp.zeros((1, LANES), f32)
    chunks = rows // CHUNK
    factors = []
    pending = None
    for c in range(chunks):
        here = slice(c * CHUNK, (c + 1) * CHUNK)
        logs = log_sums[here]
        centre = logs[CHUNK // 2 - 1 : CHUNK // 2]
        last = logs[CHUNK - 1 : CHUNK]
        outside_ref[here] = split_lanes(jnp.exp(logs - centre), heads)
        inside_ref[here] = split_lanes(jnp.exp(centre - logs) * steps[here], heads)
        offset = iota((CHUNK, LANES), 0) + c * CHUNK
        gap = distance(offset + base, lengths, FAR)
        gap_ref[here] = gap
        carried_ref[here] = split_lanes(jnp.where(gap > offset, jnp.exp(logs + total), 0.0), heads)
        if pending is not None:
            factors.append(jnp.exp(pending + centre))
        pending = last - centre
        total = total + last
    factors.append(jnp.exp(pending))
    end_gap = distance(base + rows - 1, lengths, FAR)
    decay = jnp.where(end_gap >= rows, jnp.exp(total), 0.0)
    for c in range(chunks):
        log_sums[c : c + 1] = factors[c]
    factor_ref[...] = dot(split_lanes(log_sums[0:chunks], heads), expand)
    log_sums[0:1] = decay
    log_sums[1:2] = lines_ref[2:3]
    rest_ref[...] = dot(split_lanes(log_sums[0:8], heads), expand)
    for b in range(rows // ROWS):
        here = slice(b * ROWS, (b + 1) * ROWS)
        gap = gap_ref[here]
        wide_gap = jnp.concatenate([gap] * (2 * state // LANES), 1)

        def shifted(lag):
            return packed[HALO + b * ROWS - lag : HALO + (b + 1) * ROWS - lag]

        both = convolve(shifted, taps_ref[...], wide_gap, width)
        keys, queries = both[:, :state], both[:, state:]
        query_ref[here] = queries
        offset = iota((ROWS, state), 0)
        in_chunk = offset % CHUNK
        zero = jnp.zeros_like(queries)
        kept_query_ref[here] = jnp.where(gap > in_chunk, queries.astype(f32), 0.0).astype(bf16)
        ends = jnp.zeros((ROWS, state), jnp.int32)
        for c in range(ROWS // CHUNK):
            end = base + b * ROWS + (c + 1) * CHUNK - 1
            ends = jnp.where(offset // CHUNK == c, distance(end, lengths, FAR), ends)
        last_keys = jnp.where(CHUNK - 1 - in_chunk <= ends, keys.astype(f32), 0.0)
        keys_ref[:, here] = last_keys.T.astype(bf16)
        scores = dot_nt(queries, keys)
        gap_square = jnp.concatenate([gap] * (ROWS // LANES), 1)
        scores = jnp.where(lower & (row_in - col_in <= gap_square), scores, 0.0)
        high, low = high_low(scores)
        score_high_ref[here] = high
        score_low_ref[here] = low


def scan_columns(
    shards, width,
    lengths, pick_ref, rims_ref, gap_ref, score_high_ref, score_low_ref, kept_query_ref, keys_ref,
    inside_ref, outside_ref, expand_ref, factor_ref, rest_ref, taps_ref, *refs,
):
    blocks, edge_ref = refs[:shards], refs[shards]
    out_ref, state_ref, size_ref, arrived, packed = refs[shards + 1 :]
    rows = pick_ref.shape[0]
    per = rows // shards
    base = lax.axis_index("seq") * rows
    for k in range(shards):
        arrived[k * per : (k + 1) * per] = blocks[k][...]
    packed[0:HALO] = dot(rims_ref[...], edge_ref[...])[0:HALO]
    expand = expand_ref[...]
    state_ref[...] = jnp.zeros_like(state_ref)
    for b in range(rows // ROWS):
        here = slice(b * ROWS, (b + 1) * ROWS)
        packed[HALO + b * ROWS : HALO + (b + 1) * ROWS] = dot(pick_ref[here], arrived[...])
        gap = gap_ref[here]

        def shifted(lag):
            return packed[HALO + b * ROWS - lag : HALO + (b + 1) * ROWS - lag]

        conv = convolve(shifted, taps_ref[...], jnp.concatenate([gap] * (TILE // LANES), 1), width).astype(f32)
        scaled = conv * dot(inside_ref[here], expand)
        high, low = high_low(scaled)
        score_high, score_low = score_high_ref[here], score_low_ref[here]
        total = dot(score_high, high) + dot(score_low, high) + dot(score_high, low)
        outside = dot(outside_ref[here], expand)
        carry = state_ref[...]
        parts = []
        for c in range(ROWS // CHUNK):
            inner = slice(c * CHUNK, (c + 1) * CHUNK)
            place = slice(b * ROWS + c * CHUNK, b * ROWS + (c + 1) * CHUNK)
            carry_high, carry_low = high_low(carry)
            kept = kept_query_ref[place]
            parts.append(dot(kept, carry_high) + dot(kept, carry_low))
            keys = keys_ref[:, place]
            added = dot(keys, high[inner]) + dot(keys, low[inner])
            end = base + b * ROWS + (c + 1) * CHUNK - 1
            keep = jnp.where(distance(end, lengths, FAR) >= CHUNK, 1.0, 0.0)
            number = b * (ROWS // CHUNK) + c
            carry = (carry * keep + added) * factor_ref[number : number + 1]
        state_ref[...] = carry
        out_ref[here] = outside * (total + jnp.concatenate(parts, 0)) + rest_ref[1:2] * conv
    largest = jnp.max(jnp.abs(state_ref[...]), axis=0, keepdims=True)
    size_ref[...] = jnp.broadcast_to(jnp.maximum(largest, TINY), size_ref.shape)


def gate_columns(shards, sum_ref, pick_ref, query_ref, carried_ref, expand_ref, scan_ref, state_ref, *refs):
    blocks = refs[:shards]
    out_ref, total_ref, arrived, square_ref = refs[shards:]
    rows = pick_ref.shape[0]
    per = rows // shards
    for k in range(shards):
        arrived[k * per : (k + 1) * per] = blocks[k][...]

    @pl.when(pl.program_id(0) == 0)
    def _():
        square_ref[...] = jnp.zeros_like(square_ref)

    carry_high, carry_low = high_low(state_ref[...])
    for b in range(rows // ROWS):
        here = slice(b * ROWS, (b + 1) * ROWS)
        gate = dot(pick_ref[here], arrived[...])
        queries = query_ref[here]
        earlier = dot(queries, carry_high) + dot(queries, carry_low)
        outputs = scan_ref[here] + dot(carried_ref[here], expand_ref[...]) * earlier
        gated = outputs * silu(gate)
        out_ref[here] = gated
        squares = gated * gated
        part = squares[:, :LANES]
        for piece in range(1, TILE // LANES):
            part = part + squares[:, piece * LANES : (piece + 1) * LANES]
        square_ref[here] = square_ref[here] + part

    @pl.when(pl.program_id(0) == pl.num_programs(0) - 1)
    def _():
        for b in range(rows // ROWS):
            here = slice(b * ROWS, (b + 1) * ROWS)
            total_ref[:, here] = sum_ref[:, here] + jnp.sum(square_ref[here].T, axis=0, keepdims=True)


def normalize(count, groups, *refs):
    pieces, out_ref = refs[groups + 1 : -1], refs[-1]
    gain_ref = refs[groups]
    scale = refs[0][...]
    for ref in refs[1:groups]:
        scale = scale + ref[...]
    scale = lax.rsqrt(scale / count + 1e-05)
    scale = jnp.broadcast_to(scale, (LANES, scale.shape[1])).T
    first = 0
    for ref in pieces:
        for tile in range(ref.shape[1] // LANES):
            here = slice(first + tile * LANES, first + (tile + 1) * LANES)
            value = ref[:, tile * LANES : (tile + 1) * LANES] * scale * gain_ref[:, here]
            out_ref[:, here] = value.astype(bf16)
        first += ref.shape[1]


def moved(block, axis, steps):
    count = lax.axis_size(axis)
    return lax.ppermute(block, axis, [(i, (i + steps) % count) for i in range(count)])


def after(value, *others):
    return lax.optimization_barrier((value, *others))[0]


def packed_state(state, bound):
    power = jnp.ceil(jnp.log2(bound))
    rows = jnp.broadcast_to(power, (8, state.shape[1]))
    return jnp.concatenate([state * jnp.exp2(-power), rows], 0).astype(jnp.float16)


def unpacked(packet):
    wide = packet.astype(f32)
    scale = jnp.exp2(wide[-1:])
    return wide[:-8] * scale, scale


def cut(tiles, shares):
    cuts = sorted({0, *(round(tiles * share) for share in shares), tiles})
    return list(zip(cuts, cuts[1:]))


def body(xs, gate_in, bc_in, dt_in, placement, lengths, conv_x, conv_bc, a_log, dt_bias, d_skip, norm_gain):
    shards = lax.axis_size("seq")
    groups = lax.axis_size("head")
    rows, inner = xs.shape
    width = conv_x.shape[0]
    heads = a_log.shape[0]
    head_dim = inner // heads
    state = bc_in.shape[1] // 2
    per = rows // shards
    group = per + RIM
    tiles = inner // TILE
    chunks = rows // CHUNK
    parts = cut(tiles, SHARES)
    gate_parts = cut(tiles, GATE_SHARES)
    triple = jnp.stack([dt_bias, a_log, d_skip])
    lines = jnp.pad(jnp.concatenate([triple] * GROUPS, 1), ((0, 5), (0, LANES - GROUPS * heads)))

    place = placement.reshape(1, rows)
    thin = dt_in.T
    full = rows + shards * RIM
    quarter = 2 * state // groups
    first, last = parts[0]
    sent = call(
        functools.partial(send_order, shards, width, quarter),
        [pltpu.VMEM((full, rows), bf16)]
        + [pltpu.VMEM((group, LANES), bf16)] * shards
        + [pltpu.VMEM((per, (last - first) * TILE), bf16)] * shards,
        (place, bc_in, thin, xs),
        [whole(place), whole(bc_in), whole(thin), columns(rows)],
        [whole(shape(full, rows))] + [whole(shape(group, LANES))] * shards + [columns(per)] * shards,
        grid=(last - first,),
        micros=7,
        limit=56,
    )
    picks, small, x_send = sent[0], sent[1 : 1 + shards], [sent[1 + shards :]]
    small = [small[0]] + [moved(small[k], "seq", k) for k in range(1, shards)]
    distances = list(range(shards - 1, 0, -1))
    started = []

    def queued(send, *others):
        received = [send[0]] + [None] * (shards - 1)
        for k in distances:
            waits = [started[-WINDOW]] if len(started) >= shards - 1 else []
            received[k] = moved(after(send[k], *waits, *others), "seq", k)
            started.append(received[k])
        return received

    arrived = [queued(x_send[0])]

    rims = shards * RIM
    edges = call(
        gather_rims,
        shape(rims, inner),
        (picks, xs),
        [pl.BlockSpec((rims, rows), lambda j: (rows // rims, 0)), columns(rows)],
        columns(rims),
        grid=(tiles,),
        micros=2,
    )
    edges = [edges[k * RIM : k * RIM + EDGE] for k in range(shards)]
    for k in range(1, shards):
        edges[k] = moved(after(edges[k], arrived[0][distances[0]]), "seq", k)
    edges = jnp.concatenate(edges, 0)
    small = [jnp.concatenate(small, 0)]
    mask = groups // 2
    while mask:
        held = jnp.concatenate(small, 0) if len(small) > 1 else small[0]
        small.append(lax.ppermute(held, "head", [(i, i ^ mask) for i in range(groups)]))
        mask //= 2
    for first, last in parts[1:]:
        x_send.append(
            call(
                functools.partial(gather_rows, shards),
                [shape(per, (last - first) * TILE)] * shards,
                (picks, xs),
                [whole(shape(rows, rows)), columns(rows, start=first)],
                [columns(per)] * shards,
                grid=(last - first,),
                micros=2 * (last - first),
            )
        )
    def within(first, last):
        return pl.BlockSpec((per, TILE), lambda j: (0, jnp.clip(j - first, 0, last - first - 1)))

    gate_send = call(
        functools.partial(gather_parts, shards, gate_parts),
        [shape(per, (last - first) * TILE) for first, last in gate_parts for _ in range(shards)],
        (picks, gate_in),
        [whole(shape(rows, rows)), columns(rows)],
        [within(first, last) for first, last in gate_parts for _ in range(shards)],
        grid=(tiles,),
        micros=2 * tiles,
    )
    gate_send = [gate_send[number * shards : (number + 1) * shards] for number in range(len(gate_parts))]

    kept = [
        shape(rows, rows),
        shape(RIM, shards * EDGE),
        shape(rows, LANES, dtype=jnp.int32),
        shape(rows, ROWS),
        shape(rows, ROWS),
        shape(rows, state),
        shape(rows, state),
        shape(state, rows),
        shape(rows, LANES),
        shape(rows, LANES),
        shape(rows, LANES),
        shape(LANES, inner),
        shape(chunks, inner, dtype=f32),
        shape(8, inner, dtype=f32),
    ]
    (
        pick, rims, gap, score_high, score_low, query, kept_query,
        keys, inside, outside, carried, expand, factor, rest,
    ) = call(
        functools.partial(prepare, shards, groups, width, heads, head_dim),
        kept,
        (lengths, small[0], conv_bc, lines, *small[1:]),
        [smem()] + [whole(s) for s in (small[0], conv_bc, lines, *small[1:])],
        [whole(s) for s in kept],
        scratch=[
            pltpu.VMEM((rows + HALO, 2 * state), f32),
            pltpu.VMEM((rows, LANES), f32),
            pltpu.VMEM((rows, LANES), f32),
        ],
        micros=8,
    )

    if len(parts) > 1:
        arrived.append(queued(x_send[1], gate_send[0][0], x_send[-1][0]))

    scans, ends, states, gates = [], [], [], []
    for number, part in enumerate(parts):
        blocks = arrived[number]
        first, last = part
        size = (last - first) * TILE
        if ends:
            blocks = [after(blocks[0], ends[-1])] + blocks[1:]
        scanned, local_state, largest = call(
            functools.partial(scan_columns, shards, width),
            [shape(rows, size, dtype=f32), shape(state, size, dtype=f32), shape(8, size, dtype=f32)],
            (
                lengths, pick, rims, gap, score_high, score_low, kept_query, keys, inside, outside,
                expand, factor, rest, conv_x, *blocks, edges,
            ),
            [smem()]
            + [whole(a) for a in (pick, rims, gap, score_high, score_low, kept_query, keys, inside, outside)]
            + [columns(n, start=first) for n in (LANES, chunks, 8, width)]
            + [columns(per)] * shards
            + [columns(shards * EDGE, start=first)],
            [columns(rows), columns(state), columns(8)],
            grid=(last - first,),
            scratch=[pltpu.VMEM((rows, TILE), bf16), pltpu.VMEM((rows + HALO, TILE), f32)],
            micros=5 * (last - first),
        )
        scans.append(scanned)
        ends.append(local_state)
        if number + 2 < len(parts):
            arrived.append(queued(x_send[number + 2], local_state))
        if not gates and number + 2 >= len(parts):
            gates = [queued(send, local_state) for send in gate_send]
        following = (arrived + gates)[number + 1][distances[0]]
        local_state = after(local_state, following)
        passing = rest[0:1, first * TILE : last * TILE]
        packet = None
        for step in range(1, shards):
            leaving, bound = local_state, largest[0:1]
            if packet is not None:
                incoming, reach = unpacked(packet)
                leaving, bound = leaving + passing * incoming, bound + passing * reach
            received = lax.ppermute(packed_state(leaving, bound), "seq", [(step - 1, step)])
            packet = received if packet is None else packet + received
        states.append(unpacked(packet)[0])

    outs, totals = [], [jnp.zeros((1, rows), f32)]
    for tile in range(tiles):
        part = sum(tile >= last for _, last in parts)
        gate_part = sum(tile >= last for _, last in gate_parts)
        blocks = gates[gate_part]
        if gate_part + 1 < len(gates):
            blocks = [after(blocks[0], gates[gate_part + 1][distances[0]])] + blocks[1:]
        gated, total = call(
            functools.partial(gate_columns, shards),
            [shape(rows, TILE, dtype=f32), shape(1, rows, dtype=f32)],
            (totals[-1], pick, query, carried, expand, scans[part], states[part], *blocks),
            [whole(totals[-1]), whole(pick), whole(query), whole(carried), columns(LANES, start=tile)]
            + [columns(n, start=tile - parts[part][0]) for n in (rows, state)]
            + [columns(per, start=tile - gate_parts[gate_part][0])] * shards,
            [columns(rows), whole(shape(1, rows))],
            scratch=[pltpu.VMEM((rows, TILE), bf16), pltpu.VMEM((rows, LANES), f32)],
            micros=3,
        )
        outs.append(gated)
        totals.append(total)
    total = [totals[-1]] + [moved(totals[-1], "head", k) for k in range(1, groups)]
    gain = norm_gain.reshape(1, inner)
    return call(
        functools.partial(normalize, inner * groups, groups),
        shape(rows, inner),
        (*total, gain, *outs),
        [pl.BlockSpec((1, ROWS), lambda i: (0, i))] * groups + [whole(gain)]
        + [pl.BlockSpec((ROWS, out.shape[1]), lambda i: (i, 0)) for out in outs],
        pl.BlockSpec((ROWS, inner), lambda i: (i, 0)),
        grid=(rows // ROWS,),
        micros=5,
    )


def solution(mesh):
    in_specs = (
        P(("parts", "seq"), "head"),
        P(("parts", "seq"), "head"),
        P(("parts", "seq"), None),
        P(("parts", "seq"), "head"),
        P(("parts", "seq")),
        P("parts"),
        P(None, "head"),
        P(),
        P("head"),
        P("head"),
        P("head"),
        P("head"),
    )
    out_specs = P(("parts", "seq"), "head")
    return jax.shard_map(body, mesh=mesh, in_specs=in_specs, out_specs=out_specs, check_vma=False)
```

```python
import functools

import jax
import jax.numpy as jnp
from jax import lax
from jax.experimental import pallas as pl
from jax.experimental.pallas import tpu as pltpu
from jax.sharding import PartitionSpec as P

CHUNK = 64
ROWS = 256
TILE = 256
LANES = 128
RIM = 16
EDGE = 4
SHARES = (0.4,)
GATE_SHARES = (0.6,)
WINDOW = 2
TINY = 2.0**-100
HALO = 8
GROUPS = 3
FAR = 1 << 28
FLOPS_US = 1_150_000_000
bf16 = jnp.bfloat16
f32 = jnp.float32


def dot(a, b):
    return jnp.dot(a, b, preferred_element_type=f32)


def dot_nt(a, b):
    return lax.dot_general(a, b, (((1,), (1,)), ((), ())), preferred_element_type=f32)


def iota(shape, dim):
    return lax.broadcasted_iota(jnp.int32, shape, dim)


def ones_where(mask):
    return jnp.where(mask, 1.0, 0.0).astype(bf16)


def high_low(value):
    high = value.astype(bf16)
    return high, (value - high.astype(f32)).astype(bf16)


def split_lanes(value, heads):
    lane = iota(value.shape, 1)
    high = value.astype(bf16).astype(f32)
    rest = value - high
    middle = rest.astype(bf16).astype(f32)
    lowest = rest - middle
    pieces = jnp.where(lane < heads, high, jnp.where(lane < 2 * heads, middle, lowest))
    return jnp.where(lane < GROUPS * heads, pieces, 0.0).astype(bf16)


def silu(value):
    return value * jax.nn.sigmoid(value)


def call(kernel, outs, args, in_specs, out_specs, grid=(1,), scratch=(), micros=1, limit=24):
    return pl.pallas_call(
        kernel,
        grid=grid,
        in_specs=in_specs,
        out_specs=out_specs,
        out_shape=outs,
        scratch_shapes=list(scratch),
        compiler_params=pltpu.CompilerParams(vmem_limit_bytes=limit * 1024 * 1024),
        cost_estimate=pl.CostEstimate(flops=int(micros * FLOPS_US), bytes_accessed=0, transcendentals=0),
    )(*args)


def whole(array):
    rank = len(array.shape)
    return pl.BlockSpec(array.shape, lambda *_: (0,) * rank)


def columns(rows, width=TILE, start=0):
    return pl.BlockSpec((rows, width), lambda j: (0, j + start))


def smem():
    return pl.BlockSpec(memory_space=pltpu.SMEM)


def shape(*dims, dtype=bf16):
    return jax.ShapeDtypeStruct(dims, dtype)


def send_order(shards, width, quarter, place_ref, bc_ref, dt_ref, x_ref, pick_ref, *refs):
    small_refs, x_refs = refs[:shards], refs[shards:]
    rows = place_ref.shape[1]
    per = rows // shards
    heads = dt_ref.shape[0]
    both = bc_ref.shape[1]

    @pl.when(pl.program_id(0) == 0)
    def _():
        me = lax.axis_index("seq")
        place = place_ref[...]
        padded = max(8, shards)
        owner = iota((padded, rows), 0)
        first = owner * rows
        mine = (place >= first) & (place < first + rows)
        chosen = ones_where(mine)
        earlier = ones_where(iota((LANES, LANES), 0) < iota((LANES, LANES), 1))
        before, seen = [], jnp.zeros((padded, 1), f32)
        for piece in range(rows // LANES):
            part = chosen[:, piece * LANES : (piece + 1) * LANES]
            before.append(dot(part, earlier) + seen)
            seen = seen + jnp.sum(part.astype(f32), axis=1, keepdims=True)
        before = jnp.concatenate(before, 1)
        relative = jnp.where(owner >= me, owner - me, owner - me + shards)
        target = before + (relative * per).astype(f32)
        target = jnp.sum(jnp.where(mine, target, 0.0), axis=0, keepdims=True).astype(jnp.int32)
        local = jnp.sum(jnp.where(mine, (place - first + 1).astype(f32), 0.0), axis=0, keepdims=True)
        high = jnp.floor(local * (1.0 / 64.0))
        low = local - 64.0 * high
        line = iota((LANES - quarter - heads, rows), 0)
        digits = jnp.where(line == 0, high, jnp.where(line == 1, low, 0.0)).astype(bf16)
        thin = jnp.concatenate([jnp.zeros((quarter, rows), bf16), dt_ref[...], digits], 0)
        own = lax.axis_index("head") * quarter
        lane = iota((both, LANES), 1)
        taken = ones_where((iota((both, LANES), 0) == lane + own) & (lane < quarter))
        thick = dot(bc_ref[...], taken).astype(bf16)
        for k in range(shards):
            pick = ones_where(iota((per, rows), 0) + k * per == target)
            pick_ref[k * per : (k + 1) * per] = pick
            dest = jnp.where(me + k >= shards, me + k - shards, me + k)
            row = iota((RIM, rows), 0)
            rim = ones_where((row < width - 1) & (place == row + (dest * rows - (width - 1))))
            pick_ref[rows + k * RIM : rows + (k + 1) * RIM] = rim
            small_refs[k][:per] = (dot(pick, thick) + dot_nt(pick, thin)).astype(bf16)
            small_refs[k][per:] = (dot(rim, thick) + dot_nt(rim, thin)).astype(bf16)

    gather_rows(shards, pick_ref, x_ref, *x_refs)


def gather_rows(shards, pick_ref, x_ref, *out_refs):
    rows = x_ref.shape[0]
    per = rows // shards
    values = x_ref[...]
    for k in range(shards):
        out_refs[k][...] = dot(pick_ref[k * per : (k + 1) * per], values).astype(bf16)


def gather_rims(pick_ref, x_ref, out_ref):
    out_ref[...] = dot(pick_ref[...], x_ref[...]).astype(bf16)


def gather_parts(shards, parts, pick_ref, x_ref, *out_refs):
    rows = x_ref.shape[0]
    per = rows // shards
    values = x_ref[...]
    for number, (first, last) in enumerate(parts):

        @pl.when((pl.program_id(0) >= first) & (pl.program_id(0) < last))
        def _():
            for k in range(shards):
                taken = dot(pick_ref[k * per : (k + 1) * per], values)
                out_refs[number * shards + k][...] = taken.astype(bf16)


def distance(position, lengths, limit):
    gap, start = limit, 0
    for j in range(lengths.shape[0]):
        gap = jnp.where(position >= start, jnp.minimum(gap, position - start), gap)
        start = start + lengths[j]
    return gap


def convolve(block_of, taps, gap, width):
    total = taps[0:1] * block_of(0)
    for lag in range(1, width):
        total = total + jnp.where(gap >= lag, taps[lag : lag + 1] * block_of(lag), 0.0)
    return silu(total).astype(bf16)


def prepare(
    shards, groups, width, heads, head_dim, lengths, first_ref, taps_ref, lines_ref, *refs
):
    (
        pick_ref, rims_ref, gap_ref, score_high_ref, score_low_ref, query_ref, kept_query_ref,
        keys_ref, inside_ref, outside_ref, carried_ref, expand_ref, factor_ref, rest_ref,
        packed, log_sums, steps,
    ) = refs[-17:]
    others = refs[:-17]
    rows = pick_ref.shape[0]
    per = rows // shards
    group = per + RIM
    state = query_ref.shape[1]
    base = lax.axis_index("seq") * rows
    sources = [first_ref]
    flips = [0]
    for ref in others:
        flips = flips + [flip ^ (groups // (2 * len(flips))) for flip in flips]
        sources = sources + [ref.at[n * shards * group : (n + 1) * shards * group] for n in range(len(sources))]
    quarter = 2 * state // len(sources)

    def main(ref):
        return jnp.concatenate([ref[k * group : k * group + per] for k in range(shards)], 0)

    def rim(ref):
        return jnp.concatenate([ref[k * group + per : (k + 1) * group] for k in range(shards)], 0)

    own_main = main(first_ref)
    lane = iota((8, LANES), 1)
    high_lane = quarter + heads
    weights = jnp.where(lane == high_lane, 64.0, jnp.where(lane == high_lane + 1, 1.0, 0.0)).astype(bf16)
    slots = dot_nt(weights, own_main)[0:1].astype(jnp.int32) - 1
    rim_slots = dot_nt(weights, rim(first_ref))[0:1].astype(jnp.int32) - 1 - rows + HALO
    rim_pick = ones_where(iota((RIM, shards * RIM), 0) == rim_slots)
    source, wanted = iota((shards * RIM, shards * EDGE), 0), iota((shards * RIM, shards * EDGE), 1)
    kept = ones_where((source // RIM == wanted // EDGE) & (source % RIM == wanted % EDGE))
    rims_ref[...] = dot(rim_pick, kept).astype(bf16)
    me = lax.axis_index("head")
    bc_main, bc_rim = 0.0, 0.0
    for flip, ref in zip(flips, sources):
        lane = iota((LANES, 2 * state), 0)
        spread = ones_where((lane < quarter) & (lane + (me ^ flip) * quarter == iota((LANES, 2 * state), 1)))
        bc_main = bc_main + dot(main(ref), spread)
        bc_rim = bc_rim + dot(rim(ref), spread)
    bc_main = bc_main.astype(bf16)
    packed[0:HALO] = dot(rim_pick, bc_rim.astype(bf16))[0:HALO]
    lane_of = iota((LANES, LANES), 0) - quarter
    wide = iota((LANES, LANES), 1)
    copy_dt = ones_where(
        (lane_of >= 0) & (lane_of < heads)
        & ((lane_of == wide) | (lane_of + heads == wide) | (lane_of + 2 * heads == wide))
    )
    decay_rate = -jnp.exp(lines_ref[1:2])
    row_in = iota((ROWS, ROWS), 0)
    col_in = iota((ROWS, ROWS), 1)
    same_chunk = (row_in // CHUNK) == (col_in // CHUNK)
    lower = same_chunk & (col_in <= row_in)
    sums = ones_where(lower)
    expand = iota((LANES, heads * head_dim), 0)
    head_of = jnp.where(expand >= 2 * heads, expand - 2 * heads, jnp.where(expand >= heads, expand - heads, expand))
    channel = iota((LANES, heads * head_dim), 1)
    expand = ones_where(
        (expand < GROUPS * heads) & (channel >= head_of * head_dim) & (channel < (head_of + 1) * head_dim)
    )
    expand_ref[...] = expand
    for b in range(rows // ROWS):
        here = slice(b * ROWS, (b + 1) * ROWS)
        pick = ones_where(iota((ROWS, rows), 0) + b * ROWS == slots)
        pick_ref[here] = pick
        packed[HALO + b * ROWS : HALO + (b + 1) * ROWS] = dot(pick, bc_main)
        raw = dot(pick, own_main).astype(bf16)
        step = jax.nn.softplus(dot(raw, copy_dt) + lines_ref[0:1])
        log_decay = decay_rate * step
        high = log_decay.astype(bf16)
        rest = log_decay - high.astype(f32)
        middle = rest.astype(bf16)
        lowest = (rest - middle.astype(f32)).astype(bf16)
        log_sums[here] = dot(sums, high) + dot(sums, middle) + dot(sums, lowest)
        steps[here] = step
    total = jnp.zeros((1, LANES), f32)
    chunks = rows // CHUNK
    factors = []
    pending = None
    for c in range(chunks):
        here = slice(c * CHUNK, (c + 1) * CHUNK)
        logs = log_sums[here]
        centre = logs[CHUNK // 2 - 1 : CHUNK // 2]
        last = logs[CHUNK - 1 : CHUNK]
        outside_ref[here] = split_lanes(jnp.exp(logs - centre), heads)
        inside_ref[here] = split_lanes(jnp.exp(centre - logs) * steps[here], heads)
        offset = iota((CHUNK, LANES), 0) + c * CHUNK
        gap = distance(offset + base, lengths, FAR)
        gap_ref[here] = gap
        carried_ref[here] = split_lanes(jnp.where(gap > offset, jnp.exp(logs + total), 0.0), heads)
        if pending is not None:
            factors.append(jnp.exp(pending + centre))
        pending = last - centre
        total = total + last
    factors.append(jnp.exp(pending))
    end_gap = distance(base + rows - 1, lengths, FAR)
    decay = jnp.where(end_gap >= rows, jnp.exp(total), 0.0)
    for c in range(chunks):
        log_sums[c : c + 1] = factors[c]
    factor_ref[...] = dot(split_lanes(log_sums[0:chunks], heads), expand)
    log_sums[0:1] = decay
    log_sums[1:2] = lines_ref[2:3]
    rest_ref[...] = dot(split_lanes(log_sums[0:8], heads), expand)
    for b in range(rows // ROWS):
        here = slice(b * ROWS, (b + 1) * ROWS)
        gap = gap_ref[here]
        wide_gap = jnp.concatenate([gap] * (2 * state // LANES), 1)

        def shifted(lag):
            return packed[HALO + b * ROWS - lag : HALO + (b + 1) * ROWS - lag]

        both = convolve(shifted, taps_ref[...], wide_gap, width)
        keys, queries = both[:, :state], both[:, state:]
        query_ref[here] = queries
        offset = iota((ROWS, state), 0)
        in_chunk = offset % CHUNK
        zero = jnp.zeros_like(queries)
        kept_query_ref[here] = jnp.where(gap > in_chunk, queries.astype(f32), 0.0).astype(bf16)
        ends = jnp.zeros((ROWS, state), jnp.int32)
        for c in range(ROWS // CHUNK):
            end = base + b * ROWS + (c + 1) * CHUNK - 1
            ends = jnp.where(offset // CHUNK == c, distance(end, lengths, FAR), ends)
        last_keys = jnp.where(CHUNK - 1 - in_chunk <= ends, keys.astype(f32), 0.0)
        keys_ref[:, here] = last_keys.T.astype(bf16)
        scores = dot_nt(queries, keys)
        gap_square = jnp.concatenate([gap] * (ROWS // LANES), 1)
        scores = jnp.where(lower & (row_in - col_in <= gap_square), scores, 0.0)
        high, low = high_low(scores)
        score_high_ref[here] = high
        score_low_ref[here] = low


def scan_columns(
    shards, width,
    lengths, pick_ref, rims_ref, gap_ref, score_high_ref, score_low_ref, kept_query_ref, keys_ref,
    inside_ref, outside_ref, expand_ref, factor_ref, rest_ref, taps_ref, *refs,
):
    blocks, edge_ref = refs[:shards], refs[shards]
    out_ref, state_ref, size_ref, arrived, packed = refs[shards + 1 :]
    rows = pick_ref.shape[0]
    per = rows // shards
    base = lax.axis_index("seq") * rows
    for k in range(shards):
        arrived[k * per : (k + 1) * per] = blocks[k][...]
    packed[0:HALO] = dot(rims_ref[...], edge_ref[...])[0:HALO]
    expand = expand_ref[...]
    state_ref[...] = jnp.zeros_like(state_ref)
    for b in range(rows // ROWS):
        here = slice(b * ROWS, (b + 1) * ROWS)
        packed[HALO + b * ROWS : HALO + (b + 1) * ROWS] = dot(pick_ref[here], arrived[...])
        gap = gap_ref[here]

        def shifted(lag):
            return packed[HALO + b * ROWS - lag : HALO + (b + 1) * ROWS - lag]

        conv = convolve(shifted, taps_ref[...], jnp.concatenate([gap] * (TILE // LANES), 1), width).astype(f32)
        scaled = conv * dot(inside_ref[here], expand)
        high, low = high_low(scaled)
        score_high, score_low = score_high_ref[here], score_low_ref[here]
        total = dot(score_high, high) + dot(score_low, high) + dot(score_high, low)
        outside = dot(outside_ref[here], expand)
        carry = state_ref[...]
        parts = []
        for c in range(ROWS // CHUNK):
            inner = slice(c * CHUNK, (c + 1) * CHUNK)
            place = slice(b * ROWS + c * CHUNK, b * ROWS + (c + 1) * CHUNK)
            carry_high, carry_low = high_low(carry)
            kept = kept_query_ref[place]
            parts.append(dot(kept, carry_high) + dot(kept, carry_low))
            keys = keys_ref[:, place]
            added = dot(keys, high[inner]) + dot(keys, low[inner])
            end = base + b * ROWS + (c + 1) * CHUNK - 1
            keep = jnp.where(distance(end, lengths, FAR) >= CHUNK, 1.0, 0.0)
            number = b * (ROWS // CHUNK) + c
            carry = (carry * keep + added) * factor_ref[number : number + 1]
        state_ref[...] = carry
        out_ref[here] = outside * (total + jnp.concatenate(parts, 0)) + rest_ref[1:2] * conv
    largest = jnp.max(jnp.abs(state_ref[...]), axis=0, keepdims=True)
    size_ref[...] = jnp.broadcast_to(jnp.maximum(largest, TINY), size_ref.shape)


def gate_columns(shards, sum_ref, pick_ref, query_ref, carried_ref, expand_ref, scan_ref, state_ref, *refs):
    blocks = refs[:shards]
    out_ref, total_ref, arrived, square_ref = refs[shards:]
    rows = pick_ref.shape[0]
    per = rows // shards
    for k in range(shards):
        arrived[k * per : (k + 1) * per] = blocks[k][...]

    @pl.when(pl.program_id(0) == 0)
    def _():
        square_ref[...] = jnp.zeros_like(square_ref)

    carry_high, carry_low = high_low(state_ref[...])
    for b in range(rows // ROWS):
        here = slice(b * ROWS, (b + 1) * ROWS)
        gate = dot(pick_ref[here], arrived[...])
        queries = query_ref[here]
        earlier = dot(queries, carry_high) + dot(queries, carry_low)
        outputs = scan_ref[here] + dot(carried_ref[here], expand_ref[...]) * earlier
        gated = outputs * silu(gate)
        out_ref[here] = gated
        squares = gated * gated
        part = squares[:, :LANES]
        for piece in range(1, TILE // LANES):
            part = part + squares[:, piece * LANES : (piece + 1) * LANES]
        square_ref[here] = square_ref[here] + part

    @pl.when(pl.program_id(0) == pl.num_programs(0) - 1)
    def _():
        for b in range(rows // ROWS):
            here = slice(b * ROWS, (b + 1) * ROWS)
            total_ref[:, here] = sum_ref[:, here] + jnp.sum(square_ref[here].T, axis=0, keepdims=True)


def normalize(count, groups, *refs):
    pieces, out_ref = refs[groups + 1 : -1], refs[-1]
    gain_ref = refs[groups]
    scale = refs[0][...]
    for ref in refs[1:groups]:
        scale = scale + ref[...]
    scale = lax.rsqrt(scale / count + 1e-05)
    scale = jnp.broadcast_to(scale, (LANES, scale.shape[1])).T
    first = 0
    for ref in pieces:
        for tile in range(ref.shape[1] // LANES):
            here = slice(first + tile * LANES, first + (tile + 1) * LANES)
            value = ref[:, tile * LANES : (tile + 1) * LANES] * scale * gain_ref[:, here]
            out_ref[:, here] = value.astype(bf16)
        first += ref.shape[1]


def moved(block, axis, steps):
    count = lax.axis_size(axis)
    return lax.ppermute(block, axis, [(i, (i + steps) % count) for i in range(count)])


def after(value, *others):
    return lax.optimization_barrier((value, *others))[0]


def packed_state(state, bound):
    power = jnp.ceil(jnp.log2(bound))
    rows = jnp.broadcast_to(power, (8, state.shape[1]))
    return jnp.concatenate([state * jnp.exp2(-power), rows], 0).astype(jnp.float16)


def unpacked(packet):
    wide = packet.astype(f32)
    scale = jnp.exp2(wide[-1:])
    return wide[:-8] * scale, scale


def cut(tiles, shares):
    cuts = sorted({0, *(round(tiles * share) for share in shares), tiles})
    return list(zip(cuts, cuts[1:]))


def body(xs, gate_in, bc_in, dt_in, placement, lengths, conv_x, conv_bc, a_log, dt_bias, d_skip, norm_gain):
    shards = lax.axis_size("seq")
    groups = lax.axis_size("head")
    rows, inner = xs.shape
    width = conv_x.shape[0]
    heads = a_log.shape[0]
    head_dim = inner // heads
    state = bc_in.shape[1] // 2
    per = rows // shards
    group = per + RIM
    tiles = inner // TILE
    chunks = rows // CHUNK
    parts = cut(tiles, SHARES)
    gate_parts = cut(tiles, GATE_SHARES)
    triple = jnp.stack([dt_bias, a_log, d_skip])
    lines = jnp.pad(jnp.concatenate([triple] * GROUPS, 1), ((0, 5), (0, LANES - GROUPS * heads)))

    place = placement.reshape(1, rows)
    thin = dt_in.T
    full = rows + shards * RIM
    quarter = 2 * state // groups
    first, last = parts[0]
    sent = call(
        functools.partial(send_order, shards, width, quarter),
        [pltpu.VMEM((full, rows), bf16)]
        + [pltpu.VMEM((group, LANES), bf16)] * shards
        + [pltpu.VMEM((per, (last - first) * TILE), bf16)] * shards,
        (place, bc_in, thin, xs),
        [whole(place), whole(bc_in), whole(thin), columns(rows)],
        [whole(shape(full, rows))] + [whole(shape(group, LANES))] * shards + [columns(per)] * shards,
        grid=(last - first,),
        micros=7,
        limit=56,
    )
    picks, small, x_send = sent[0], sent[1 : 1 + shards], [sent[1 + shards :]]
    small = [small[0]] + [moved(small[k], "seq", k) for k in range(1, shards)]
    distances = list(range(shards - 1, 0, -1))
    started = []

    def queued(send, *others):
        received = [send[0]] + [None] * (shards - 1)
        for k in distances:
            waits = [started[-WINDOW]] if len(started) >= shards - 1 else []
            received[k] = moved(after(send[k], *waits, *others), "seq", k)
            started.append(received[k])
        return received

    arrived = [queued(x_send[0])]

    rims = shards * RIM
    edges = call(
        gather_rims,
        shape(rims, inner),
        (picks, xs),
        [pl.BlockSpec((rims, rows), lambda j: (rows // rims, 0)), columns(rows)],
        columns(rims),
        grid=(tiles,),
        micros=2,
    )
    edges = [edges[k * RIM : k * RIM + EDGE] for k in range(shards)]
    for k in range(1, shards):
        edges[k] = moved(after(edges[k], arrived[0][distances[0]]), "seq", k)
    edges = jnp.concatenate(edges, 0)
    small = [jnp.concatenate(small, 0)]
    mask = groups // 2
    while mask:
        held = jnp.concatenate(small, 0) if len(small) > 1 else small[0]
        small.append(lax.ppermute(held, "head", [(i, i ^ mask) for i in range(groups)]))
        mask //= 2
    for first, last in parts[1:]:
        x_send.append(
            call(
                functools.partial(gather_rows, shards),
                [shape(per, (last - first) * TILE)] * shards,
                (picks, xs),
                [whole(shape(rows, rows)), columns(rows, start=first)],
                [columns(per)] * shards,
                grid=(last - first,),
                micros=2 * (last - first),
            )
        )
    def within(first, last):
        return pl.BlockSpec((per, TILE), lambda j: (0, jnp.clip(j - first, 0, last - first - 1)))

    gate_send = call(
        functools.partial(gather_parts, shards, gate_parts),
        [shape(per, (last - first) * TILE) for first, last in gate_parts for _ in range(shards)],
        (picks, gate_in),
        [whole(shape(rows, rows)), columns(rows)],
        [within(first, last) for first, last in gate_parts for _ in range(shards)],
        grid=(tiles,),
        micros=2 * tiles,
    )
    gate_send = [gate_send[number * shards : (number + 1) * shards] for number in range(len(gate_parts))]

    kept = [
        shape(rows, rows),
        shape(RIM, shards * EDGE),
        shape(rows, LANES, dtype=jnp.int32),
        shape(rows, ROWS),
        shape(rows, ROWS),
        shape(rows, state),
        shape(rows, state),
        shape(state, rows),
        shape(rows, LANES),
        shape(rows, LANES),
        shape(rows, LANES),
        shape(LANES, inner),
        shape(chunks, inner, dtype=f32),
        shape(8, inner, dtype=f32),
    ]
    (
        pick, rims, gap, score_high, score_low, query, kept_query,
        keys, inside, outside, carried, expand, factor, rest,
    ) = call(
        functools.partial(prepare, shards, groups, width, heads, head_dim),
        kept,
        (lengths, small[0], conv_bc, lines, *small[1:]),
        [smem()] + [whole(s) for s in (small[0], conv_bc, lines, *small[1:])],
        [whole(s) for s in kept],
        scratch=[
            pltpu.VMEM((rows + HALO, 2 * state), f32),
            pltpu.VMEM((rows, LANES), f32),
            pltpu.VMEM((rows, LANES), f32),
        ],
        micros=8,
    )

    if len(parts) > 1:
        arrived.append(queued(x_send[1], gate_send[0][0], x_send[-1][0]))

    scans, ends, states, gates = [], [], [], []
    for number, part in enumerate(parts):
        blocks = arrived[number]
        first, last = part
        size = (last - first) * TILE
        if ends:
            blocks = [after(blocks[0], ends[-1])] + blocks[1:]
        scanned, local_state, largest = call(
            functools.partial(scan_columns, shards, width),
            [shape(rows, size, dtype=f32), shape(state, size, dtype=f32), shape(8, size, dtype=f32)],
            (
                lengths, pick, rims, gap, score_high, score_low, kept_query, keys, inside, outside,
                expand, factor, rest, conv_x, *blocks, edges,
            ),
            [smem()]
            + [whole(a) for a in (pick, rims, gap, score_high, score_low, kept_query, keys, inside, outside)]
            + [columns(n, start=first) for n in (LANES, chunks, 8, width)]
            + [columns(per)] * shards
            + [columns(shards * EDGE, start=first)],
            [columns(rows), columns(state), columns(8)],
            grid=(last - first,),
            scratch=[pltpu.VMEM((rows, TILE), bf16), pltpu.VMEM((rows + HALO, TILE), f32)],
            micros=5 * (last - first),
        )
        scans.append(scanned)
        ends.append(local_state)
        if number + 2 < len(parts):
            arrived.append(queued(x_send[number + 2], local_state))
        if not gates and number + 2 >= len(parts):
            gates = [queued(send, local_state) for send in gate_send]
        following = (arrived + gates)[number + 1][distances[0]]
        local_state = after(local_state, following)
        passing = rest[0:1, first * TILE : last * TILE]
        packet = None
        for step in range(1, shards):
            leaving, bound = local_state, largest[0:1]
            if packet is not None:
                incoming, reach = unpacked(packet)
                leaving, bound = leaving + passing * incoming, bound + passing * reach
            received = lax.ppermute(packed_state(leaving, bound), "seq", [(step - 1, step)])
            packet = received if packet is None else packet + received
        states.append(unpacked(packet)[0])

    outs, totals = [], [jnp.zeros((1, rows), f32)]
    bounds = sorted({bound for pair in parts + gate_parts for bound in pair})
    for first, last in zip(bounds, bounds[1:]):
        part = sum(first >= end for _, end in parts)
        gate_part = sum(first >= end for _, end in gate_parts)
        blocks = gates[gate_part]
        if gate_part + 1 < len(gates):
            blocks = [after(blocks[0], gates[gate_part + 1][distances[0]])] + blocks[1:]
        gated, total = call(
            functools.partial(gate_columns, shards),
            [shape(rows, (last - first) * TILE, dtype=f32), shape(1, rows, dtype=f32)],
            (totals[-1], pick, query, carried, expand, scans[part], states[part], *blocks),
            [whole(totals[-1]), whole(pick), whole(query), whole(carried), columns(LANES, start=first)]
            + [columns(n, start=first - parts[part][0]) for n in (rows, state)]
            + [columns(per, start=first - gate_parts[gate_part][0])] * shards,
            [columns(rows), whole(shape(1, rows))],
            grid=(last - first,),
            scratch=[pltpu.VMEM((rows, TILE), bf16), pltpu.VMEM((rows, LANES), f32)],
            micros=3 * (last - first),
        )
        outs.append(gated)
        totals.append(total)
    total = [totals[-1]] + [moved(totals[-1], "head", k) for k in range(1, groups)]
    gain = norm_gain.reshape(1, inner)
    return call(
        functools.partial(normalize, inner * groups, groups),
        shape(rows, inner),
        (*total, gain, *outs),
        [pl.BlockSpec((1, ROWS), lambda i: (0, i))] * groups + [whole(gain)]
        + [pl.BlockSpec((ROWS, out.shape[1]), lambda i: (i, 0)) for out in outs],
        pl.BlockSpec((ROWS, inner), lambda i: (i, 0)),
        grid=(rows // ROWS,),
        micros=5,
    )


def solution(mesh):
    in_specs = (
        P(("parts", "seq"), "head"),
        P(("parts", "seq"), "head"),
        P(("parts", "seq"), None),
        P(("parts", "seq"), "head"),
        P(("parts", "seq")),
        P("parts"),
        P(None, "head"),
        P(),
        P("head"),
        P("head"),
        P("head"),
        P("head"),
    )
    out_specs = P(("parts", "seq"), "head")
    return jax.shard_map(body, mesh=mesh, in_specs=in_specs, out_specs=out_specs, check_vma=False)
```
